32 devices in a mesh: groups: 2 (over y), dp: 4 (over z), replica: 4 (over x, core).
Axes of the slice: x: 2, y: 2, z: 4, core: 2. Of those that a mesh axis runs over, the one named last changes fastest.
Arguments:
- embeddings: bfloat16 [32768, 768], P(('groups', 'dp', 'replica')), parts along dimension 0, may hold values from -8 to 8
- codes: int32 [32768, 96], P(('groups', 'dp', 'replica')), parts along dimension 0, may hold values from 0 to 255
- rotation: bfloat16 [1536, 768], P('groups'), parts along dimension 0, may hold values from -2 to 2
- codebook: bfloat16 [512, 768], P(('groups', 'dp')), parts along dimension 0, may hold values from -8 to 8
Outputs:
- new_codebook: float32 [512, 768], P(('groups', 'dp')), parts along dimension 0
- cross: float32 [1536, 768], P(('groups', 'dp')), parts along dimension 0
The draws below stay inside these ranges and needn't reach their ends.
There are 2 independent parts, one for each index of `groups`. The reference program is written for one: setup_inputs(seed, part) draws one part's arguments, and reference() takes and returns one part's arrays. A program takes and returns all parts, laid end to end along the dimension named above; each array names one. Nothing has to cross between parts.
All inputs are finite; a program needn't handle non-finite values.
Results may differ from the reference program's by a relative error of at most 0.00044.
Values may be sent and summed in bfloat16 or wider, within the bound.
No kernel may reach another device: no remote copies, remote signals or barrier semaphores. Data moves between devices by JAX's collectives and lax.ppermute only.
A program may use at most 64 MiB of HBM per device.

```python
import jax
import jax.numpy as jnp
from jax import lax

D = 768
SUB = 96
KW = 256
SD = 8
TOTAL = 16384


def shared_codes(key):
    return jax.random.randint(jax.random.fold_in(key, 901), (TOTAL, SUB), 0, KW, dtype=jnp.int32)


def shared_table(key):
    return jnp.clip(jax.random.normal(jax.random.fold_in(key, 900), (KW, D), jnp.float32), -4.0, 4.0)


def draw_codes(key, part):
    return shared_codes(key)


def draw_embeddings(key, part):
    labels = shared_codes(key)
    table = shared_table(key).reshape(KW, SUB, SD)
    key = jax.random.fold_in(key, 11)
    base = table[labels, jnp.arange(SUB, dtype=jnp.int32)[None, :]].reshape(TOTAL, D)
    noise = 0.6 * jax.random.normal(key, (TOTAL, D), jnp.float32)
    return jnp.clip(base + noise, -8.0, 8.0).astype(jnp.bfloat16)


def draw_codebook(key, part):
    table = shared_table(key)
    key = jax.random.fold_in(key, 12)
    noise = 0.4 * jax.random.normal(key, (KW, D), jnp.float32)
    return jnp.clip(table + noise, -8.0, 8.0).astype(jnp.bfloat16)


def draw_rotation(key, part):
    key = jax.random.fold_in(key, 13)
    noise = jnp.clip(jax.random.normal(key, (D, D), jnp.float32), -6.0, 6.0) * 0.5
    eye = (jnp.arange(D)[:, None] == jnp.arange(D)[None, :]).astype(jnp.float32)
    return (eye + noise / jnp.sqrt(jnp.float32(D))).astype(jnp.bfloat16)


def setup_inputs(seed: int = 0, part: int = 0) -> dict:
    arg_keys = jax.random.split(jax.random.key(seed), 5)
    part_keys = jax.random.split(jax.random.fold_in(arg_keys[4], part), 5)
    return {
        "embeddings": draw_embeddings(jax.random.fold_in(jax.random.fold_in(arg_keys[4], part), 71), part),
        "codes": draw_codes(jax.random.fold_in(jax.random.fold_in(arg_keys[4], part), 71), part),
        "rotation": draw_rotation(jax.random.fold_in(jax.random.fold_in(arg_keys[4], part), 71), part),
        "codebook": draw_codebook(jax.random.fold_in(jax.random.fold_in(arg_keys[4], part), 71), part),
    }


prior_count = 4.0


def reference(embeddings, codes, rotation, codebook):
    rotated = jnp.dot(embeddings, rotation, preferred_element_type=jnp.float32).astype(jnp.bfloat16)
    book_three = codebook.reshape(KW, SUB, SD)
    recon = book_three[codes, jnp.arange(SUB, dtype=jnp.int32)[None, :]].reshape(TOTAL, D)
    cross = lax.dot_general(embeddings, recon, (((0,), (0,)), ((), ())), preferred_element_type=jnp.float32) / TOTAL
    rot_split = rotated.astype(jnp.float32).reshape(TOTAL, SUB, SD).transpose(1, 0, 2)
    code_split = codes.T

    def per_subspace(pair):
        values, labels = pair
        summed = jax.ops.segment_sum(values, labels, num_segments=KW)
        counted = jax.ops.segment_sum(jnp.ones(labels.shape, jnp.float32), labels, num_segments=KW)
        return summed, counted

    sums, counts = lax.map(per_subspace, (rot_split, code_split))
    sums = sums.transpose(1, 0, 2).reshape(KW, D)
    counts = jnp.repeat(counts.T, SD, axis=1)
    new_codebook = (sums + prior_count * codebook.astype(jnp.float32)) / (counts + prior_count)
    return new_codebook, cross
```

```python
import jax
import jax.numpy as jnp
from jax import lax
from jax.experimental import pallas as pl
from jax.experimental.pallas import tpu as pltpu
from jax.sharding import PartitionSpec as P

prior_count = 4.0
lane = 128
fine = 64
pack = 4
level = 32000.0
octave = 8.0
pad = 16

f32, bf16, i32, i16 = jnp.float32, jnp.bfloat16, jnp.int32, jnp.int16
nt = (((1,), (1,)), ((), ()))


def call(kernel, outs, args, scratch, name):
    return pl.pallas_call(
        kernel,
        out_shape=outs,
        scratch_shapes=scratch,
        compiler_params=pltpu.CompilerParams(vmem_limit_bytes=48 << 20),
        name=name,
    )(*args)


def my_half(width):
    core = lax.axis_index("replica") % 2
    return core, pl.ds(pl.multiple_of(core * width, lane), width)


def quantize(x):
    top = jnp.maximum(jnp.max(jnp.abs(x), axis=0, keepdims=True), 1e-30)
    power = jnp.ceil(jnp.log2(top) * octave)
    terms = jnp.round(x * (level * jnp.exp2(power * (-1.0 / octave)))).astype(i32)
    powers = jnp.broadcast_to(power.astype(i32), (pad, x.shape[1]))
    return jnp.concatenate([terms, powers], axis=0).astype(i16)


def dequantize(q):
    rows = q.shape[0] - pad
    power = q[rows:].astype(f32)[:1]
    return q[:rows].astype(f32) * (jnp.exp2(power * (1.0 / octave)) * (1.0 / level))


def sums_kernel(shape, e0, e1, c0, c1, rot, *rest):
    rows, half, n_sub, n_words, n_out = shape
    outs, (codes_out, turned, rt, lhs, rhs, total) = rest[:n_out], rest[n_out:]
    core, cols = my_half(half)
    subs = n_sub // 2
    for i, c in enumerate((c0, c1)):
        turned[...] = c[...].T
        codes_out[:, i * rows : (i + 1) * rows] = turned[pl.ds(pl.multiple_of(core * subs, 16), subs), :]
    rot_t = rot[:, cols].T
    for i, e in enumerate((e0, e1)):
        rt[:, i * rows : (i + 1) * rows] = lax.dot_general(
            rot_t, e[...], nt, preferred_element_type=f32
        ).astype(bf16)
    width = 2 * rows
    coarse = n_words // fine
    groups = subs // pack
    block = groups * 8 + 16
    row8 = lax.broadcasted_iota(i32, (8, width), 0)
    rowf = lax.broadcasted_iota(i32, (fine, width), 0).astype(bf16)
    out_lane = lax.broadcasted_iota(i32, (8, pack * fine), 1)
    for g in range(groups):
        b = g % 2
        high = []
        for s in range(pack):
            code = jnp.broadcast_to(codes_out[g * pack + s : g * pack + s + 1, :], (8, width))
            high.append(code // fine)
            low = (code % fine).astype(f32)
            low = jnp.concatenate([low] * (fine // 8), axis=0).astype(bf16)
            rhs[b, s * fine : (s + 1) * fine, :] = jnp.where(low == rowf, 1.0, 0.0).astype(bf16)
        for p in range(pack // 2):
            pair = jnp.concatenate([high[2 * p], high[2 * p + 1]], axis=0).astype(f32).astype(bf16)
            r = rt[g * pack * 8 + p * 16 : g * pack * 8 + (p + 1) * 16, :]
            for h in range(coarse):
                at = h * pack * 8 + p * 16
                lhs[b, at : at + 16, :] = jnp.where(pair == h, r, 0.0).astype(bf16)
        ones = []
        for p in range(pack // 2):
            both = jnp.where(row8 < coarse, high[2 * p], high[2 * p + 1])
            ones.append(jnp.where(both == row8 % coarse, 1.0, 0.0))
        base = coarse * pack * 8
        lhs[b, base : base + 16, :] = jnp.concatenate(ones, axis=0).astype(bf16)
        got = lax.dot_general(lhs[b], rhs[b], nt, preferred_element_type=f32)
        for h in range(coarse):
            kept = got[h * 32 : h * 32 + 8]
            for s in range(1, pack):
                kept = jnp.where(out_lane // fine == s, got[h * 32 + s * 8 : h * 32 + s * 8 + 8], kept)
            total[h * block + g * 8 : h * block + g * 8 + 8, :] = kept
        row = lax.broadcasted_iota(i32, (16, pack * fine), 0)
        lanes = lax.broadcasted_iota(i32, (16, pack * fine), 1)
        counts = jnp.where(row // coarse == lanes // fine, got[base : base + 16], 0.0)
        counts = counts[:8] + counts[8:]
        counts = counts[:coarse] + counts[coarse:]
        for h in range(coarse):
            at = h * block + groups * 8 + g
            total[at : at + 1, :] = counts[h : h + 1]
    zero = jnp.zeros((16 - groups, pack * fine), f32)
    for h in range(coarse):
        total[h * block + groups * 8 + groups : (h + 1) * block, :] = zero
    if n_out == 1:
        outs[0][...] = total[...]
    else:
        me = lax.axis_index("dp")
        for k in range(n_out):
            to = lax.rem(me + k, n_out)
            outs[k][...] = total[pl.ds(pl.multiple_of(to * block, 16), block), :]


def cross_kernel(shape, e0, e1, codes, *rest):
    rows, half, n_words, n_book, n_out = shape
    books, outs, (book, recon, total) = rest[:n_book], rest[n_book : n_book + n_out], rest[n_book + n_out :]
    me = lax.axis_index("dp")
    owned = n_words // n_book
    for k in range(n_book):
        source = lax.rem(me + n_book - k, n_book) if n_book > 1 else 0
        book[pl.ds(pl.multiple_of(source * owned, owned), owned), :] = books[k][...].astype(f32)
    table = book[...].T
    width = 2 * rows
    for p in range(half // 16):
        made = []
        for s in (2 * p, 2 * p + 1):
            code = jnp.broadcast_to(codes[s : s + 1, :], (8, width))
            parts = []
            for at in range(0, width, lane):
                c = code[:, at : at + lane]
                index = c % lane
                value = None
                for t in range(0, n_words, lane):
                    found = jnp.take_along_axis(
                        table[s * 8 : s * 8 + 8, t : t + lane], index, axis=1, mode="promise_in_bounds"
                    )
                    value = found if value is None else jnp.where(c >= t, found, value)
                parts.append(value)
            made.append(jnp.concatenate(parts, axis=1))
        recon[p * 16 : (p + 1) * 16, :] = jnp.concatenate(made, axis=0).astype(bf16)
    turned = jnp.dot(recon[:, :rows], e0[...], preferred_element_type=f32)
    turned += jnp.dot(recon[:, rows:], e1[...], preferred_element_type=f32)
    if n_out == 1:
        outs[0][...] = turned.T
    else:
        total[...] = turned.T
        block = total.shape[0] // n_out
        for k in range(n_out):
            to = lax.rem(me + k, n_out)
            terms = total[pl.ds(pl.multiple_of(to * block, 16), block), :]
            outs[k][...] = quantize(terms) if k else terms


def add_cross_kernel(own, *rest):
    total = own[...]
    for q in rest[:-1]:
        total += dequantize(q[...])
    rest[-1][...] = quantize(total)


def add_sums_kernel(*refs):
    total = refs[0][...]
    for r in refs[1:-1]:
        total += r[...]
    refs[-1][...] = total


def finish_cross_kernel(scale, q0, q1, p0, p1, out):
    half = q0.shape[1]
    core, mine = my_half(half)
    other = pl.ds(pl.multiple_of((1 - core) * half, lane), half)
    out[:, mine] = (dequantize(q0[...]) + dequantize(q1[...])) * scale
    out[:, other] = (dequantize(p0[...]) + dequantize(p1[...])) * scale


def finish_book_kernel(q0, q1, p0, p1, codebook, out, turned):
    half = codebook.shape[1] // 2
    core, mine = my_half(half)
    other = pl.ds(pl.multiple_of((1 - core) * half, lane), half)
    groups = half // (8 * pack)
    for cols, a, b in ((mine, q0, q1), (other, p0, p1)):
        s = a[...] + b[...]
        for g in range(groups):
            sums = s[g * 8 : g * 8 + 8]
            counts = jnp.broadcast_to(s[groups * 8 + g : groups * 8 + g + 1], sums.shape)
            for j in range(pack):
                at = (g * pack + j) * 8
                cut = slice(j * fine, (j + 1) * fine)
                turned[at : at + 8, :] = jnp.concatenate([sums[:, cut], counts[:, cut]], axis=1)
        t = turned[...].T
        old = codebook[:, cols].astype(f32)
        out[:, cols] = (t[:fine] + prior_count * old) / (t[fine:] + prior_count)


def local(embeddings, codes, rotation, codebook):
    rows, width = embeddings.shape
    n_sub = codes.shape[1]
    half = width // 2
    n = lax.axis_size("dp")
    replicas = lax.axis_size("replica")
    n_words = codebook.shape[0] * n
    owned = codebook.shape[0]
    out_rows = width // n
    core = lax.axis_index("replica") % 2
    direct = owned == fine and replicas == 4

    def swap(x, bit):
        return lax.ppermute(x, "replica", [(i, i ^ bit) for i in range(replicas)])

    def send(x, k):
        return lax.ppermute(x, "dp", [(i, (i + k) % n) for i in range(n)])

    book = lax.dynamic_slice_in_dim(codebook, core * half, half, 1)
    if direct:
        books = [book] + [send(book, k) for k in range(1, n)]
    else:
        books = [lax.all_gather(book, "dp", axis=0, tiled=True)]
    e1 = swap(embeddings, 1)
    c1 = swap(codes, 1)
    n_out = n if direct else 1
    coarse = n_words // fine
    groups = n_sub // 2 // pack
    block = groups * 8 + 16
    lhs_rows = coarse * pack * 8 + 16
    *sums, codes_t = call(
        lambda *refs: sums_kernel((rows, half, n_sub, n_words, n_out), *refs),
        [jax.ShapeDtypeStruct((coarse * block // n_out, pack * fine), f32)] * n_out
        + [jax.ShapeDtypeStruct((n_sub // 2, 2 * rows), i32)],
        (embeddings, e1, codes, c1, rotation),
        [
            pltpu.VMEM((n_sub, rows), i32),
            pltpu.VMEM((half, 2 * rows), bf16),
            pltpu.VMEM((2, lhs_rows, 2 * rows), bf16),
            pltpu.VMEM((2, pack * fine, 2 * rows), bf16),
            pltpu.VMEM((coarse * block, pack * fine), f32),
        ],
        "codeword_sums",
    )
    if direct:
        cross_outs = [jax.ShapeDtypeStruct((out_rows, half), f32)]
        cross_outs += [jax.ShapeDtypeStruct((out_rows + pad, half), i16)] * (n - 1)
    else:
        cross_outs = [jax.ShapeDtypeStruct((width, half), f32)]
    cross = call(
        lambda *refs: cross_kernel((rows, half, n_words, len(books), n_out), *refs),
        cross_outs,
        (embeddings, e1, codes_t, *books),
        [
            pltpu.VMEM((n_words, half), f32),
            pltpu.VMEM((half, 2 * rows), bf16),
            pltpu.VMEM((width, half), f32),
        ],
        "cross_terms",
    )
    scale = 1.0 / (rows * n * replicas)
    if not direct:
        return plain_finish(sums[0], cross[0], codebook, n_words, scale, swap)

    sums = [sums[0]] + [send(sums[k], k) for k in range(1, n)]
    cross = [cross[0]] + [send(cross[k], k) for k in range(1, n)]
    q = call(add_sums_kernel, jax.ShapeDtypeStruct((block, pack * fine), f32), sums, [], "add_sums")
    q1 = swap(q, 2)
    p, p1 = swap(q, 1), swap(q1, 1)
    new_codebook = call(
        finish_book_kernel,
        jax.ShapeDtypeStruct(codebook.shape, f32),
        (q, q1, p, p1, codebook),
        [pltpu.VMEM((half, lane), f32)],
        "finish_book",
    )
    t = call(add_cross_kernel, jax.ShapeDtypeStruct((out_rows + pad, half), i16), cross, [], "add_cross")
    t1 = swap(t, 2)
    u, u1 = swap(t, 1), swap(t1, 1)
    cross_out = call(
        lambda *refs: finish_cross_kernel(scale, *refs),
        jax.ShapeDtypeStruct((out_rows, width), f32),
        (t, t1, u, u1),
        [],
        "finish_cross",
    )
    return new_codebook, cross_out


def plain_finish(sums, cross, codebook, n_words, scale, swap):
    half = cross.shape[1]
    coarse = n_words // fine
    groups = half // (8 * pack)
    sums = sums.reshape(coarse, groups * 8 + 16, pack * fine)
    counts = sums[:, groups * 8 : groups * 8 + groups].reshape(coarse, groups, pack, fine)
    counts = counts.transpose(0, 3, 1, 2).reshape(n_words, groups * pack)
    sums = sums[:, : groups * 8].reshape(coarse, groups, 8, pack, fine)
    sums = sums.transpose(0, 4, 1, 3, 2).reshape(n_words, half)
    parts = []
    for x in (sums, counts, cross):
        x = lax.psum_scatter(x, "dp", scatter_dimension=0, tiled=True)
        bit = 2
        while bit < lax.axis_size("replica"):
            x = x + swap(x, bit)
            bit *= 2
        y = swap(x, 1)
        first = lax.axis_index("replica") % 2 == 0
        parts.append(jnp.where(first, jnp.concatenate([x, y], 1), jnp.concatenate([y, x], 1)))
    sums, counts, cross = parts
    spread = jnp.repeat(counts, 8, axis=1)
    new_codebook = (sums + prior_count * codebook.astype(f32)) / (spread + prior_count)
    return new_codebook, cross * scale


def solution(mesh):
    in_specs = (
        P(("groups", "dp", "replica"), None),
        P(("groups", "dp", "replica"), None),
        P("groups", None),
        P(("groups", "dp"), None),
    )
    out_specs = (P(("groups", "dp"), None), P(("groups", "dp"), None))
    return jax.shard_map(local, mesh=mesh, in_specs=in_specs, out_specs=out_specs, check_vma=False)
```

```python
import jax
import jax.numpy as jnp
from jax import lax
from jax.experimental import pallas as pl
from jax.experimental.pallas import tpu as pltpu
from jax.sharding import PartitionSpec as P

prior_count = 4.0
lane = 128
hops = (2, 1, 3)
fine = 64
pack = 4
level = 32000.0
octave = 8.0
pad = 16

f32, bf16, i32, i16 = jnp.float32, jnp.bfloat16, jnp.int32, jnp.int16
nt = (((1,), (1,)), ((), ()))


def call(kernel, outs, args, scratch, name, flops=0, unread=(), hbm=()):
    spaces = [pl.ANY if i in unread + hbm else pltpu.VMEM for i in range(len(args))]
    args = [pltpu.with_memory_space_constraint(x, pltpu.HBM) if i in hbm else x for i, x in enumerate(args)]
    shapes = jax.tree.leaves(outs) + list(args)
    bytes_accessed = sum(s.size * s.dtype.itemsize for s in shapes)
    return pl.pallas_call(
        kernel,
        out_shape=outs,
        in_specs=[pl.BlockSpec(memory_space=space) for space in spaces],
        scratch_shapes=scratch,
        compiler_params=pltpu.CompilerParams(vmem_limit_bytes=20 << 20),
        cost_estimate=pl.CostEstimate(flops=flops, bytes_accessed=bytes_accessed, transcendentals=0),
        name=name,
    )(*args)


def my_half(width):
    core = lax.axis_index("replica") % 2
    return core, pl.ds(pl.multiple_of(core * width, lane), width)


def powers_of(x):
    top = jnp.maximum(jnp.max(jnp.abs(x), axis=0, keepdims=True), 1e-30)
    return jnp.ceil(jnp.log2(top) * octave)


def units(power):
    return level * jnp.exp2(power * (-1.0 / octave))


def scales(power):
    return jnp.exp2(power * (1.0 / octave)) * (1.0 / level)


def quantize(x):
    power = powers_of(x)
    terms = jnp.round(x * units(power)).astype(i32)
    powers = jnp.broadcast_to(power.astype(i32), (pad, x.shape[1]))
    return jnp.concatenate([terms, powers], axis=0).astype(i16)


def dequantize(q):
    rows = q.shape[0] - pad
    return q[:rows].astype(f32) * scales(q[rows:].astype(f32)[:1])


def quantize_sums(x, groups):
    tail = groups * 8
    sums, powers = [], []
    for g in range(groups):
        s = x[g * 8 : g * 8 + 8]
        powers.append(powers_of(s))
        sums.append(jnp.round(s * units(powers[-1])))
    return jnp.concatenate(sums + powers + [x[tail + groups :]], axis=0).astype(i32).astype(i16)


def dequantize_sums(q, groups):
    x = q.astype(f32)
    tail = groups * 8
    sums = [x[g * 8 : g * 8 + 8] * scales(x[tail + g : tail + g + 1]) for g in range(groups)]
    return jnp.concatenate(sums + [x[tail:]], axis=0)


def block_rows(groups):
    return groups * 8 + -(-2 * groups // 16) * 16


def begin_kernel(shape, e0, e1, c0, c1, rot, out, codes, rt, v0, rot_half, lhs, rhs, total, sems):
    rows, half, n_words, n_out = shape
    subs = codes.shape[0]
    core, cols = my_half(half)
    mine = pl.ds(pl.multiple_of(core * subs, 16), subs)
    loads = [
        pltpu.make_async_copy(rot.at[:, cols], rot_half, sems.at[0]),
        pltpu.make_async_copy(c0.at[mine, :], codes.at[:, :rows], sems.at[1]),
        pltpu.make_async_copy(e0, v0, sems.at[2]),
    ]
    for load in loads:
        load.start()
    codes[:, rows:] = c1[mine, :]
    loads[0].wait()
    rot_t = rot_half[...].T
    rt[:, rows:] = lax.dot_general(rot_t, e1[...], nt, preferred_element_type=f32).astype(bf16)
    loads[1].wait()
    loads[2].wait()
    rt[:, :rows] = lax.dot_general(rot_t, v0[...], nt, preferred_element_type=f32).astype(bf16)
    x = lax.axis_index("replica") // 2
    half_sums(0 if n_out == 1 else 1 - x, n_words, codes, rt, lhs, rhs, total)
    if n_out == 1:
        out[...] = total[...]
        return
    me = lax.axis_index("dp")
    block = total.shape[0] // n_out
    for k in range(n_out):
        at = pl.ds(pl.multiple_of((me ^ k) * block, 16), block)
        out[k * block : (k + 1) * block, :] = quantize_sums(total[at, :], subs // pack // 2)


def cross_kernel(shape, e0, e1, codes, *rest):
    rows, half, n_words, n_book, n_out = shape
    books, outs, (book, recon, turned, total) = rest[:n_book], rest[n_book : n_book + n_out], rest[n_book + n_out :]
    me = lax.axis_index("dp")
    owned = n_words // n_book
    for k in range(n_book):
        book[pl.ds(pl.multiple_of((me ^ k) * owned if n_book > 1 else 0, owned), owned), :] = books[k][...].astype(f32)
    table = book[...].T
    for part in range(half // lane):
        for p in range(part * lane // 16, (part + 1) * lane // 16):
            made = []
            for s in (2 * p, 2 * p + 1):
                parts = []
                for at in range(0, 2 * rows, lane):
                    c = jnp.broadcast_to(codes[s : s + 1, at : at + lane], (8, lane))
                    index = c & (lane - 1)
                    value = None
                    for t in range(0, n_words, lane):
                        found = jnp.take_along_axis(
                            table[s * 8 : s * 8 + 8, t : t + lane], index, axis=1, mode="promise_in_bounds"
                        )
                        value = found if value is None else jnp.where(c >= t, found, value)
                    parts.append(value)
                made.append(jnp.concatenate(parts, axis=1))
            recon[p * 16 : (p + 1) * 16, :] = jnp.concatenate(made, axis=0).astype(bf16)
        cut = slice(part * lane, (part + 1) * lane)
        got = jnp.dot(recon[cut, :rows], e0[...], preferred_element_type=f32)
        turned[cut, :] = got + jnp.dot(recon[cut, rows:], e1[...], preferred_element_type=f32)
    if n_out == 1:
        outs[0][...] = turned[...].T
    else:
        total[...] = turned[...].T
        block = total.shape[0] // n_out
        for k in range(n_out):
            terms = total[pl.ds(pl.multiple_of((me ^ k) * block, 16), block), :]
            outs[k][...] = quantize(terms) if k else terms


def half_sums(part, n_words, codes, rt, lhs, rhs, total):
    width = codes.shape[1]
    coarse = n_words // fine
    shift = fine.bit_length() - 1
    low_mask, coarse_shift = fine - 1, coarse.bit_length() - 1
    groups = codes.shape[0] // pack // 2
    block = block_rows(groups)
    subs = groups * pack
    codes = codes[pl.ds(pl.multiple_of(part * subs, 8), subs), :]
    row8 = lax.broadcasted_iota(i32, (8, width), 0)
    row16 = lax.broadcasted_iota(i32, (16, width), 0)
    steps = [(row16 + 16 * t).astype(f32).astype(bf16) for t in range(fine // 16)]
    one, zero = jnp.ones((16, width), bf16), jnp.zeros((16, width), bf16)
    out_sub = lax.broadcasted_iota(i32, (8, pack * fine), 1) >> shift
    count_row = lax.broadcasted_iota(i32, (16, pack * fine), 0) >> coarse_shift
    count_sub = lax.broadcasted_iota(i32, (16, pack * fine), 1) >> shift
    total[...] = jnp.zeros_like(total)
    for g in range(groups):
        b = g % 2
        high = []
        for s in range(pack):
            code = jnp.broadcast_to(codes[g * pack + s : g * pack + s + 1, :], (8, width))
            high.append(code >> shift)
            low = (code & low_mask).astype(f32)
            low = jnp.concatenate([low, low], axis=0).astype(bf16)
            for t, step in enumerate(steps):
                at = s * fine + t * 16
                rhs[b, at : at + 16, :] = jnp.where(low == step, one, zero)
        for p in range(pack // 2):
            pair = jnp.concatenate([high[2 * p], high[2 * p + 1]], axis=0).astype(f32).astype(bf16)
            r = rt[pl.ds(pl.multiple_of((part * subs + g * pack + 2 * p) * 8, 16), 16), :]
            for h in range(coarse):
                at = h * pack * 8 + p * 16
                lhs[b, at : at + 16, :] = jnp.where(pair == h, r, zero)
        ones = []
        for p in range(pack // 2):
            both = jnp.where(row8 < coarse, high[2 * p], high[2 * p + 1])
            ones.append(jnp.where(both == (row8 & (coarse - 1)), 1.0, 0.0))
        base = coarse * pack * 8
        lhs[b, base : base + 16, :] = jnp.concatenate(ones, axis=0).astype(bf16)
        got = lax.dot_general(lhs[b], rhs[b], nt, preferred_element_type=f32)
        counts = jnp.where(count_row == count_sub, got[base : base + 16], 0.0)
        counts = counts[:8] + counts[8:]
        counts = counts[:coarse] + counts[coarse:]
        for h in range(coarse):
            kept = got[h * 32 : h * 32 + 8]
            for s in range(1, pack):
                kept = jnp.where(out_sub == s, got[h * 32 + s * 8 : h * 32 + s * 8 + 8], kept)
            at = h * block
            total[at + g * 8 : at + g * 8 + 8, :] = kept
            at += groups * 9 + g
            total[at : at + 1, :] = counts[h : h + 1]


def sums_kernel(shape, codes, rt, got, _, *rest):
    n_words, n_out = shape
    outs, (lhs, rhs, total) = rest[:-3], rest[-3:]
    half_sums(1 if n_out == 1 else lax.axis_index("replica") // 2, n_words, codes, rt, lhs, rhs, total)
    if n_out == 1:
        outs[0][...] = total[...]
        return
    me = lax.axis_index("dp")
    block = total.shape[0] // n_out
    groups = codes.shape[0] // pack // 2
    for k in range(n_out):
        at = pl.ds(pl.multiple_of((me ^ k) * block, 16), block)
        x = total[at, :] + dequantize_sums(got[k * block : (k + 1) * block, :], groups)
        outs[k][...] = quantize_sums(x, groups)


def tiles(x):
    return [x[:, at : at + lane] for at in range(0, x.shape[1], lane)]


def add_kernel(groups, n, *refs):
    cross, sums, out = refs[:n], refs[n : 2 * n], refs[-1]
    total = cross[0][...]
    for q in cross[1:]:
        total += dequantize(q[...])
    parts = tiles(quantize(total))
    total = dequantize_sums(sums[0][...], groups)
    for r in sums[1:]:
        total += dequantize_sums(r[...], groups)
    parts += tiles(quantize_sums(total, groups))
    out[...] = jnp.concatenate(parts, axis=0)


def finish_kernel(scale, shape, q0, q1, p0, p1, codebook, out, cross, turned):
    terms, block = shape
    width = codebook.shape[1]
    half = width // 2
    core = lax.axis_index("replica") % 2
    low = lax.axis_index("replica") < 2
    groups = half // (8 * pack) // 2
    for start, m0, m1 in ((core * half, q0, q1), (half - core * half, p0, p1)):
        start = pl.multiple_of(start, lane)
        across = half // lane
        for j in range(across):
            at = slice(j * terms, (j + 1) * terms)
            cross[:, pl.ds(start + j * lane, lane)] = (dequantize(m0[at, :]) + dequantize(m1[at, :])) * scale
        wide = pack * fine // lane
        subs = pack // wide
        for j in range(wide):
            at = slice(across * terms + j * block, across * terms + (j + 1) * block)
            a, b = dequantize_sums(m0[at, :], groups), dequantize_sums(m1[at, :], groups)
            for part, x in enumerate((jnp.where(low, a, b), jnp.where(low, b, a))):
                for g in range(groups):
                    sums = x[g * 8 : g * 8 + 8]
                    row = groups * 9 + g
                    counts = jnp.broadcast_to(x[row : row + 1], sums.shape)
                    for i in range(subs):
                        to = ((part * groups + g) * pack + j * subs + i) * 8
                        cut = slice(i * fine, (i + 1) * fine)
                        turned[to : to + 8, :] = jnp.concatenate([sums[:, cut], counts[:, cut]], axis=1)
        t = turned[...].T
        cols = pl.ds(start, half)
        old = codebook[:, cols].astype(f32)
        out[:, cols] = (t[:fine] + prior_count * old) / (t[fine:] + prior_count)


def local(embeddings, codes, rotation, codebook):
    rows, width = embeddings.shape
    n_sub = codes.shape[1]
    half = width // 2
    n = lax.axis_size("dp")
    replicas = lax.axis_size("replica")
    n_words = codebook.shape[0] * n
    owned = codebook.shape[0]
    out_rows = width // n
    core = lax.axis_index("replica") % 2
    direct = n == 4 and owned == fine and replicas == 4 and rows * n * replicas < 32768

    def swap(x, bit):
        return lax.ppermute(x, "replica", [(i, i ^ bit) for i in range(replicas)])

    def send(blocks):
        sent = {k: lax.ppermute(blocks[k], "dp", [(i, i ^ k) for i in range(n)]) for k in hops}
        return [blocks[0]] + [sent[k] for k in range(1, n)]

    e1 = swap(embeddings, 1)
    c0 = codes.T
    c1 = swap(c0, 1)
    book = lax.dynamic_slice_in_dim(codebook, core * half, half, 1)
    if direct:
        books = send([book] * n)
    else:
        books = [lax.all_gather(book, "dp", axis=0, tiled=True)]
    n_out = n if direct else 1
    coarse = n_words // fine
    groups = n_sub // 2 // pack // 2
    block = block_rows(groups)
    lhs_rows = coarse * pack * 8 + 16
    if direct:
        cross_outs = [jax.ShapeDtypeStruct((out_rows, half), f32)]
        cross_outs += [jax.ShapeDtypeStruct((out_rows + pad, half), i16)] * (n - 1)
    else:
        cross_outs = [jax.ShapeDtypeStruct((width, half), f32)]
    sums_shape = (coarse * block, pack * fine)
    buffers = [
        pltpu.VMEM((2, lhs_rows, 2 * rows), bf16),
        pltpu.VMEM((2, pack * fine, 2 * rows), bf16),
        pltpu.VMEM(sums_shape, f32),
    ]
    first, my_codes, rt, e0 = call(
        lambda *refs: begin_kernel((rows, half, n_words, n_out), *refs),
        [
            jax.ShapeDtypeStruct(sums_shape, i16 if direct else f32),
            jax.ShapeDtypeStruct((n_sub // 2, 2 * rows), i32),
            jax.ShapeDtypeStruct((half, 2 * rows), bf16),
            jax.ShapeDtypeStruct(embeddings.shape, bf16),
        ],
        (embeddings, e1, c0, c1, rotation),
        [pltpu.VMEM((width, half), bf16), *buffers, pltpu.SemaphoreType.DMA((3,))],
        "begin",
        flops=8 * rows * half * width,
        hbm=(0, 2, 4),
    )
    cross = call(
        lambda *refs: cross_kernel((rows, half, n_words, len(books), n_out), *refs),
        cross_outs,
        (e0, e1, my_codes, *books),
        [
            pltpu.VMEM((n_words, half), f32),
            pltpu.VMEM((half, 2 * rows), bf16),
            pltpu.VMEM((half, width), f32),
            pltpu.VMEM((width, half), f32),
        ],
        "cross_terms",
        flops=4 * rows * half * width,
    )
    scale = 1.0 / (rows * n * replicas)
    got = swap(first, 2) if direct else first
    sums = call(
        lambda *refs: sums_kernel((n_words, n_out), *refs),
        [jax.ShapeDtypeStruct((block, pack * fine), i16)] * n if direct else [jax.ShapeDtypeStruct(sums_shape, f32)],
        (my_codes, rt, got, cross[0]),
        buffers,
        "codeword_sums",
        flops=8 * rows * half * width,
        unread=(3,),
    )
    if not direct:
        return plain_finish((first, sums[0]), cross[0], codebook, n_words, scale, swap)

    cross, sums = send(cross), send(sums)
    size = (out_rows + pad) * half // lane + block * pack * fine // lane
    q = call(
        lambda *refs: add_kernel(groups, n, *refs),
        jax.ShapeDtypeStruct((size, lane), i16),
        (*cross, *sums),
        [],
        "add",
    )
    q1 = swap(q, 2)
    return call(
        lambda *refs: finish_kernel(scale, (out_rows + pad, block), *refs),
        [jax.ShapeDtypeStruct(codebook.shape, f32), jax.ShapeDtypeStruct((out_rows, width), f32)],
        (q, q1, swap(q, 1), swap(q1, 1), codebook),
        [pltpu.VMEM((half, lane), f32)],
        "finish",
    )


def plain_finish(sums, cross, codebook, n_words, scale, swap):
    half = cross.shape[1]
    coarse = n_words // fine
    groups = half // (8 * pack) // 2
    sums = jnp.stack([x.reshape(coarse, -1, pack * fine) for x in sums])
    counts = sums[:, :, groups * 9 : groups * 10].reshape(2, coarse, groups, pack, fine)
    counts = counts.transpose(1, 4, 0, 2, 3).reshape(n_words, half // 8)
    sums = sums[:, :, : groups * 8].reshape(2, coarse, groups, 8, pack, fine)
    sums = sums.transpose(1, 5, 0, 2, 4, 3).reshape(n_words, half)
    parts = []
    for x in (sums, counts, cross):
        x = lax.psum_scatter(x, "dp", scatter_dimension=0, tiled=True)
        bit = 2
        while bit < lax.axis_size("replica"):
            x = x + swap(x, bit)
            bit *= 2
        y = swap(x, 1)
        first = lax.axis_index("replica") % 2 == 0
        parts.append(jnp.where(first, jnp.concatenate([x, y], 1), jnp.concatenate([y, x], 1)))
    sums, counts, cross = parts
    spread = jnp.repeat(counts, 8, axis=1)
    new_codebook = (sums + prior_count * codebook.astype(f32)) / (spread + prior_count)
    return new_codebook, cross * scale


def solution(mesh):
    in_specs = (
        P(("groups", "dp", "replica"), None),
        P(("groups", "dp", "replica"), None),
        P("groups", None),
        P(("groups", "dp"), None),
    )
    out_specs = (P(("groups", "dp"), None), P(("groups", "dp"), None))
    return jax.shard_map(local, mesh=mesh, in_specs=in_specs, out_specs=out_specs, check_vma=False)
```

```python
import jax
import jax.numpy as jnp
from jax import lax
from jax.experimental import pallas as pl
from jax.experimental.pallas import tpu as pltpu
from jax.sharding import PartitionSpec as P

prior_count = 4.0
lane = 128
hops = (2, 3, 1)
fine = 64
pack = 4
level = 32000.0
octave = 8.0
pad = 16

f32, bf16, i32, i16 = jnp.float32, jnp.bfloat16, jnp.int32, jnp.int16
nt = (((1,), (1,)), ((), ()))


def call(kernel, outs, args, scratch, name, flops=0, unread=(), hbm=()):
    spaces = [pl.ANY if i in unread + hbm else pltpu.VMEM for i in range(len(args))]
    args = [pltpu.with_memory_space_constraint(x, pltpu.HBM) if i in hbm else x for i, x in enumerate(args)]
    shapes = jax.tree.leaves(outs) + list(args)
    bytes_accessed = sum(s.size * s.dtype.itemsize for s in shapes)
    return pl.pallas_call(
        kernel,
        out_shape=outs,
        in_specs=[pl.BlockSpec(memory_space=space) for space in spaces],
        scratch_shapes=scratch,
        compiler_params=pltpu.CompilerParams(vmem_limit_bytes=20 << 20),
        cost_estimate=pl.CostEstimate(flops=flops, bytes_accessed=bytes_accessed, transcendentals=0),
        name=name,
    )(*args)


def my_half(width):
    core = lax.axis_index("replica") % 2
    return core, pl.ds(pl.multiple_of(core * width, lane), width)


def powers_of(x):
    top = jnp.maximum(jnp.max(jnp.abs(x), axis=0, keepdims=True), 1e-30)
    return jnp.ceil(jnp.log2(top) * octave)


def units(power):
    return level * jnp.exp2(power * (-1.0 / octave))


def scales(power):
    return jnp.exp2(power * (1.0 / octave)) * (1.0 / level)


def tiles(x):
    return [x[:, at : at + lane] for at in range(0, x.shape[1], lane)]


def whole(x):
    return x.astype(i32).astype(i16)


def encode(x):
    power = powers_of(x)
    return tiles(jnp.round(x * units(power))), tiles(power)


def decode(x, rows, powers):
    parts = [x[j * rows : (j + 1) * rows] * scales(powers[j : j + 1]) for j in range(powers.shape[0])]
    return jnp.concatenate(parts, axis=1)


def encode_sums(x, groups):
    tail = groups * 8
    sums, powers = [], []
    for g in range(groups):
        s = x[g * 8 : g * 8 + 8]
        powers.append(powers_of(s))
        sums.append(jnp.round(s * units(powers[-1])))
    return jnp.concatenate(sums + powers + [x[tail + groups :]], axis=0)


def decode_sums(x, groups):
    tail = groups * 8
    sums = [x[g * 8 : g * 8 + 8] * scales(x[tail + g : tail + g + 1]) for g in range(groups)]
    return jnp.concatenate(sums + [x[tail:]], axis=0)


def with_rows(tile, rows, groups):
    at = groups * 10
    return jnp.concatenate([tile[:at], *rows, tile[at + len(rows) :]], axis=0)


def block_rows(groups):
    return groups * 8 + -(-2 * groups // 16) * 16


def begin_kernel(shape, e0, e1, c0, c1, rot, out, codes, rt, v0, rot_half, lhs, rhs, total, sems):
    rows, half, n_words, n_out = shape
    subs = codes.shape[0]
    core, cols = my_half(half)
    mine = pl.ds(pl.multiple_of(core * subs, 16), subs)
    loads = [
        pltpu.make_async_copy(rot.at[:, cols], rot_half, sems.at[0]),
        pltpu.make_async_copy(c0.at[mine, :], codes.at[:, :rows], sems.at[1]),
        pltpu.make_async_copy(e0, v0, sems.at[2]),
    ]
    for load in loads:
        load.start()
    codes[:, rows:] = c1[mine, :]
    loads[0].wait()
    rot_t = rot_half[...].T
    rt[:, rows:] = lax.dot_general(rot_t, e1[...], nt, preferred_element_type=f32).astype(bf16)
    loads[1].wait()
    loads[2].wait()
    rt[:, :rows] = lax.dot_general(rot_t, v0[...], nt, preferred_element_type=f32).astype(bf16)
    x = lax.axis_index("replica") // 2
    half_sums(0 if n_out == 1 else 1 - x, n_words, codes, rt, lhs, rhs, total)
    if n_out == 1:
        out[...] = total[...]
        return
    me = lax.axis_index("dp")
    block = total.shape[0] // n_out
    for k in range(n_out):
        at = pl.ds(pl.multiple_of((me ^ k) * block, 16), block)
        out[k * block : (k + 1) * block, :] = encode_sums(total[at, :], subs // pack // 2)


def cross_kernel(shape, e0, e1, codes, first, *rest):
    rows, half, n_words, n_book, n_out = shape
    books, outs, (book, recon, turned, total) = rest[:n_book], rest[n_book:-4], rest[-4:]
    me = lax.axis_index("dp")
    owned = n_words // n_book
    for i, k in enumerate((0,) + hops if n_book > 1 else (0,)):
        book[pl.ds(pl.multiple_of((me ^ k) * owned if n_book > 1 else 0, owned), owned), :] = books[i][...].astype(f32)
    table = book[...].T
    for part in range(half // lane):
        for p in range(part * lane // 16, (part + 1) * lane // 16):
            made = []
            for s in (2 * p, 2 * p + 1):
                parts = []
                for at in range(0, 2 * rows, lane):
                    c = jnp.broadcast_to(codes[s : s + 1, at : at + lane], (8, lane))
                    index = c & (lane - 1)
                    value = None
                    for t in range(0, n_words, lane):
                        found = jnp.take_along_axis(
                            table[s * 8 : s * 8 + 8, t : t + lane], index, axis=1, mode="promise_in_bounds"
                        )
                        value = found if value is None else jnp.where(c >= t, found, value)
                    parts.append(value)
                made.append(jnp.concatenate(parts, axis=1))
            recon[p * 16 : (p + 1) * 16, :] = jnp.concatenate(made, axis=0).astype(bf16)
        cut = slice(part * lane, (part + 1) * lane)
        got = jnp.dot(recon[cut, :rows], e0[...], preferred_element_type=f32)
        turned[cut, :] = got + jnp.dot(recon[cut, rows:], e1[...], preferred_element_type=f32)
    if n_out == 1:
        outs[0][...] = turned[...].T
        outs[1][...] = first[...]
        return
    total[...] = turned[...].T
    own, own_late, message, *sent = outs
    block, sums = total.shape[0] // n_out, first.shape[0] // n_out
    early, late = block // 2, block // 4
    groups = codes.shape[0] // pack // 2
    x = lax.axis_index("replica") // 2
    for k in range(n_out):
        at = (me ^ k) * block
        terms = total[pl.ds(pl.multiple_of(at, 16), early), :]
        if k:
            parts, powers = encode(terms)
            powers.append(jnp.zeros((pad - len(powers), lane), f32))
            sent[hops.index(k)][...] = whole(jnp.concatenate(parts + powers, axis=0))
        else:
            own[...] = terms
        mine = pl.ds(pl.multiple_of(at + early + x * late, 16), late)
        other = pl.ds(pl.multiple_of(at + early + (1 - x) * late, 16), late)
        own_late[k * late : (k + 1) * late, :] = total[mine, :]
        parts, powers = encode(total[other, :])
        low, high = tiles(first[k * sums : (k + 1) * sums, :])
        size = message.shape[0] // n_out
        message[k * size : (k + 1) * size, :] = whole(
            jnp.concatenate(parts + [with_rows(low, powers, groups), high], axis=0)
        )


def half_sums(part, n_words, codes, rt, lhs, rhs, total):
    width = codes.shape[1]
    coarse = n_words // fine
    shift = fine.bit_length() - 1
    low_mask, coarse_shift = fine - 1, coarse.bit_length() - 1
    groups = codes.shape[0] // pack // 2
    block = block_rows(groups)
    subs = groups * pack
    codes = codes[pl.ds(pl.multiple_of(part * subs, 8), subs), :]
    row8 = lax.broadcasted_iota(i32, (8, width), 0)
    row16 = lax.broadcasted_iota(i32, (16, width), 0)
    steps = [(row16 + 16 * t).astype(f32).astype(bf16) for t in range(fine // 16)]
    one, zero = jnp.ones((16, width), bf16), jnp.zeros((16, width), bf16)
    out_sub = lax.broadcasted_iota(i32, (8, pack * fine), 1) >> shift
    count_row = lax.broadcasted_iota(i32, (16, pack * fine), 0) >> coarse_shift
    count_sub = lax.broadcasted_iota(i32, (16, pack * fine), 1) >> shift
    total[...] = jnp.zeros_like(total)
    for g in range(groups):
        b = g % 2
        high = []
        for s in range(pack):
            code = jnp.broadcast_to(codes[g * pack + s : g * pack + s + 1, :], (8, width))
            high.append(code >> shift)
            low = (code & low_mask).astype(f32)
            low = jnp.concatenate([low, low], axis=0).astype(bf16)
            for t, step in enumerate(steps):
                at = s * fine + t * 16
                rhs[b, at : at + 16, :] = jnp.where(low == step, one, zero)
        for p in range(pack // 2):
            pair = jnp.concatenate([high[2 * p], high[2 * p + 1]], axis=0).astype(f32).astype(bf16)
            r = rt[pl.ds(pl.multiple_of((part * subs + g * pack + 2 * p) * 8, 16), 16), :]
            for h in range(coarse):
                at = h * pack * 8 + p * 16
                lhs[b, at : at + 16, :] = jnp.where(pair == h, r, zero)
        ones = []
        for p in range(pack // 2):
            both = jnp.where(row8 < coarse, high[2 * p], high[2 * p + 1])
            ones.append(jnp.where(both == (row8 & (coarse - 1)), 1.0, 0.0))
        base = coarse * pack * 8
        lhs[b, base : base + 16, :] = jnp.concatenate(ones, axis=0).astype(bf16)
        got = lax.dot_general(lhs[b], rhs[b], nt, preferred_element_type=f32)
        counts = jnp.where(count_row == count_sub, got[base : base + 16], 0.0)
        counts = counts[:8] + counts[8:]
        counts = counts[:coarse] + counts[coarse:]
        for h in range(coarse):
            kept = got[h * 32 : h * 32 + 8]
            for s in range(1, pack):
                kept = jnp.where(out_sub == s, got[h * 32 + s * 8 : h * 32 + s * 8 + 8], kept)
            at = h * block
            total[at + g * 8 : at + g * 8 + 8, :] = kept
            at += groups * 9 + g
            total[at : at + 1, :] = counts[h : h + 1]


def sums_kernel(fixed, codes, rt, _, out, lhs, rhs, total):
    n_words, direct = fixed
    half_sums(lax.axis_index("replica") // 2 if direct else 1, n_words, codes, rt, lhs, rhs, total)
    out[...] = total[...]


def open_late(x, rows, across, groups):
    at = rows * across
    low, high = x[at : at + (x.shape[0] - at) // 2], x[at + (x.shape[0] - at) // 2 :]
    powers = low[groups * 10 : groups * 10 + across]
    return decode(x, rows, powers), jnp.concatenate([decode_sums(low, groups), decode_sums(high, groups)], axis=1)


def add_half_kernel(groups, own_late, own_sums, got, *outs):
    me = lax.axis_index("dp")
    n = len(outs)
    late, block, size = own_late.shape[0] // n, own_sums.shape[0] // n, got.shape[0] // n
    across = own_late.shape[1] // lane
    for i, k in enumerate((0,) + hops):
        cross, sums = open_late(got[k * size : (k + 1) * size, :].astype(f32), late, across, groups)
        parts, powers = encode(own_late[k * late : (k + 1) * late, :] + cross)
        sums += own_sums[pl.ds(pl.multiple_of((me ^ k) * block, 16), block), :]
        low, high = tiles(encode_sums(sums, groups))
        outs[i][...] = whole(jnp.concatenate(parts + [with_rows(low, powers, groups), high], axis=0))


def add_kernel(groups, n, *refs):
    (own, *early), late, out = refs[:n], refs[n : 2 * n], refs[-1]
    total = own[...]
    rows, across = total.shape[0], total.shape[1] // lane
    for q in early:
        x = q[...].astype(f32)
        total += decode(x, rows, x[rows * across : rows * across + across])
    parts, powers = encode(total)
    cross = sums = None
    for q in late:
        c, s = open_late(q[...].astype(f32), rows // 2, across, groups)
        cross, sums = (c, s) if cross is None else (cross + c, sums + s)
    late_parts, late_powers = encode(cross)
    low, high = tiles(encode_sums(sums, groups))
    low, high = with_rows(low, late_powers, groups), with_rows(high, powers, groups)
    out[...] = whole(jnp.concatenate(parts + late_parts + [low, high], axis=0))


def finish_kernel(scale, early, q0, q1, p0, p1, codebook, out, cross, turned):
    late = early // 2
    width = codebook.shape[1]
    half = width // 2
    across = half // lane
    core = lax.axis_index("replica") % 2
    low = lax.axis_index("replica") < 2
    groups = half // (8 * pack) // 2
    for start, m0, m1 in ((core * half, q0, q1), (half - core * half, p0, p1)):
        cols = pl.ds(pl.multiple_of(start, lane), half)
        opened = []
        for m in (m0, m1):
            x = m[...].astype(f32)
            late_cross, sums = open_late(x[early * across :], late, across, groups)
            at = x.shape[0] - sums.shape[0] + groups * 10
            opened.append((decode(x, early, x[at : at + across]), late_cross, sums))
        (a, b), lates, halves = zip(*opened)
        cross[:early, cols] = (a + b) * scale
        for part, (a, b) in enumerate((lates, lates[::-1])):
            cross[early + part * late : early + (part + 1) * late, cols] = jnp.where(low, a, b) * scale
        for part, (a, b) in enumerate((halves, halves[::-1])):
            x = jnp.where(low, a, b)
            for g in range(groups):
                sums = x[g * 8 : g * 8 + 8]
                row = groups * 9 + g
                counts = jnp.broadcast_to(x[row : row + 1], sums.shape)
                for i in range(pack):
                    to = ((part * groups + g) * pack + i) * 8
                    cut = slice(i * fine, (i + 1) * fine)
                    turned[to : to + 8, :] = jnp.concatenate([sums[:, cut], counts[:, cut]], axis=1)
        t = turned[...].T
        old = codebook[:, cols].astype(f32)
        out[:, cols] = (t[:fine] + prior_count * old) / (t[fine:] + prior_count)


def local(embeddings, codes, rotation, codebook):
    rows, width = embeddings.shape
    n_sub = codes.shape[1]
    half = width // 2
    n = lax.axis_size("dp")
    replicas = lax.axis_size("replica")
    n_words = codebook.shape[0] * n
    owned = codebook.shape[0]
    out_rows = width // n
    core = lax.axis_index("replica") % 2
    direct = n == 4 and owned == fine and replicas == 4 and rows * n * replicas < 32768

    def swap(x, bit):
        return lax.ppermute(x, "replica", [(i, i ^ bit) for i in range(replicas)])

    def exchange(blocks):
        return [lax.ppermute(x, "dp", [(i, i ^ k) for i in range(n)]) for k, x in zip(hops, blocks)]

    e1 = swap(embeddings, 1)
    c0 = codes.T
    c1 = swap(c0, 1)
    book = lax.dynamic_slice_in_dim(codebook, core * half, half, 1)
    if direct:
        books = [book] + exchange([book] * len(hops))
    else:
        books = [lax.all_gather(book, "dp", axis=0, tiled=True)]
    n_out = n if direct else 1
    coarse = n_words // fine
    groups = n_sub // 2 // pack // 2
    block = block_rows(groups)
    lhs_rows = coarse * pack * 8 + 16
    sums_shape = (coarse * block, pack * fine)
    buffers = [
        pltpu.VMEM((2, lhs_rows, 2 * rows), bf16),
        pltpu.VMEM((2, pack * fine, 2 * rows), bf16),
        pltpu.VMEM(sums_shape, f32),
    ]
    first, my_codes, rt, e0 = call(
        lambda *refs: begin_kernel((rows, half, n_words, n_out), *refs),
        [
            jax.ShapeDtypeStruct(sums_shape, f32),
            jax.ShapeDtypeStruct((n_sub // 2, 2 * rows), i32),
            jax.ShapeDtypeStruct((half, 2 * rows), bf16),
            jax.ShapeDtypeStruct(embeddings.shape, bf16),
        ],
        (embeddings, e1, c0, c1, rotation),
        [pltpu.VMEM((width, half), bf16), *buffers, pltpu.SemaphoreType.DMA((3,))],
        "begin",
        flops=8 * rows * half * width,
        hbm=(0, 2, 4),
    )
    early, late = out_rows // 2, out_rows // 4
    across = half // lane
    late_size = late * across + block * pack * fine // lane
    if direct:
        cross_outs = [
            jax.ShapeDtypeStruct((early, half), f32),
            jax.ShapeDtypeStruct((n * late, half), f32),
            jax.ShapeDtypeStruct((n * late_size, lane), i16),
        ] + [jax.ShapeDtypeStruct((early * across + pad, lane), i16)] * (n - 1)
    else:
        cross_outs = [jax.ShapeDtypeStruct((width, half), f32), jax.ShapeDtypeStruct(first.shape, f32)]
    cross = call(
        lambda *refs: cross_kernel((rows, half, n_words, len(books), n_out), *refs),
        cross_outs,
        (e0, e1, my_codes, first, *books),
        [
            pltpu.VMEM((n_words, half), f32),
            pltpu.VMEM((half, 2 * rows), bf16),
            pltpu.VMEM((half, width), f32),
            pltpu.VMEM((width, half), f32),
        ],
        "cross_terms",
        flops=4 * rows * half * width,
    )
    scale = 1.0 / (rows * n * replicas)
    own = call(
        lambda *refs: sums_kernel((n_words, direct), *refs),
        jax.ShapeDtypeStruct(sums_shape, f32),
        (my_codes, rt, cross[0]),
        buffers,
        "codeword_sums",
        flops=8 * rows * half * width,
        unread=(2,),
    )
    if not direct:
        return plain_finish((cross[1], own), cross[0], codebook, n_words, scale, swap)

    own_early, own_late, message, *early_sent = cross
    late_blocks = call(
        lambda *refs: add_half_kernel(groups, *refs),
        [jax.ShapeDtypeStruct((late_size, lane), i16)] * n,
        (own_late, own, swap(message, 2)),
        [],
        "add_half",
    )
    q = call(
        lambda *refs: add_kernel(groups, n, *refs),
        jax.ShapeDtypeStruct((early * across + late_size, lane), i16),
        (own_early, *exchange(early_sent), late_blocks[0], *exchange(late_blocks[1:])),
        [],
        "add",
    )
    q1 = swap(q, 2)
    return call(
        lambda *refs: finish_kernel(scale, early, *refs),
        [jax.ShapeDtypeStruct(codebook.shape, f32), jax.ShapeDtypeStruct((out_rows, width), f32)],
        (q, q1, swap(q, 1), swap(q1, 1), codebook),
        [pltpu.VMEM((half, lane), f32)],
        "finish",
    )


def plain_finish(sums, cross, codebook, n_words, scale, swap):
    half = cross.shape[1]
    coarse = n_words // fine
    groups = half // (8 * pack) // 2
    sums = jnp.stack([x.reshape(coarse, -1, pack * fine) for x in sums])
    counts = sums[:, :, groups * 9 : groups * 10].reshape(2, coarse, groups, pack, fine)
    counts = counts.transpose(1, 4, 0, 2, 3).reshape(n_words, half // 8)
    sums = sums[:, :, : groups * 8].reshape(2, coarse, groups, 8, pack, fine)
    sums = sums.transpose(1, 5, 0, 2, 4, 3).reshape(n_words, half)
    parts = []
    for x in (sums, counts, cross):
        x = lax.psum_scatter(x, "dp", scatter_dimension=0, tiled=True)
        bit = 2
        while bit < lax.axis_size("replica"):
            x = x + swap(x, bit)
            bit *= 2
        y = swap(x, 1)
        first = lax.axis_index("replica") % 2 == 0
        parts.append(jnp.where(first, jnp.concatenate([x, y], 1), jnp.concatenate([y, x], 1)))
    sums, counts, cross = parts
    spread = jnp.repeat(counts, 8, axis=1)
    new_codebook = (sums + prior_count * codebook.astype(f32)) / (spread + prior_count)
    return new_codebook, cross * scale


def solution(mesh):
    in_specs = (
        P(("groups", "dp", "replica"), None),
        P(("groups", "dp", "replica"), None),
        P("groups", None),
        P(("groups", "dp"), None),
    )
    out_specs = (P(("groups", "dp"), None), P(("groups", "dp"), None))
    return jax.shard_map(local, mesh=mesh, in_specs=in_specs, out_specs=out_specs, check_vma=False)
```

```python
import jax
import jax.numpy as jnp
from jax import lax
from jax.experimental import pallas as pl
from jax.experimental.pallas import tpu as pltpu
from jax.sharding import PartitionSpec as P

prior_count = 4.0
lane = 128
hops = (2, 3, 1)
fine = 64
pack = 4
level = 32000.0
octave = 8.0
pad = 16

f32, bf16, i32, i16 = jnp.float32, jnp.bfloat16, jnp.int32, jnp.int16
nt = (((1,), (1,)), ((), ()))


def call(kernel, outs, args, scratch, name, flops=0, unread=(), hbm=()):
    spaces = [pl.ANY if i in unread + hbm else pltpu.VMEM for i in range(len(args))]
    args = [pltpu.with_memory_space_constraint(x, pltpu.HBM) if i in hbm else x for i, x in enumerate(args)]
    shapes = jax.tree.leaves(outs) + list(args)
    bytes_accessed = sum(s.size * s.dtype.itemsize for s in shapes)
    return pl.pallas_call(
        kernel,
        out_shape=outs,
        in_specs=[pl.BlockSpec(memory_space=space) for space in spaces],
        scratch_shapes=scratch,
        compiler_params=pltpu.CompilerParams(vmem_limit_bytes=20 << 20),
        cost_estimate=pl.CostEstimate(flops=flops, bytes_accessed=bytes_accessed, transcendentals=0),
        name=name,
    )(*args)


def my_half(width):
    core = lax.axis_index("replica") % 2
    return core, pl.ds(pl.multiple_of(core * width, lane), width)


def powers_of(x):
    top = jnp.maximum(jnp.max(jnp.abs(x), axis=0, keepdims=True), 1e-30)
    return jnp.ceil(jnp.log2(top) * octave)


def units(power):
    return level * jnp.exp2(power * (-1.0 / octave))


def scales(power):
    return jnp.exp2(power * (1.0 / octave)) * (1.0 / level)


def tiles(x):
    return [x[:, at : at + lane] for at in range(0, x.shape[1], lane)]


def whole(x):
    return x.astype(i32).astype(i16)


def encode(x):
    power = powers_of(x)
    return tiles(jnp.round(x * units(power))), tiles(power)


def decode(x, rows, powers):
    parts = [x[j * rows : (j + 1) * rows] * scales(powers[j : j + 1]) for j in range(powers.shape[0])]
    return jnp.concatenate(parts, axis=1)


def encode_sums(x, groups):
    tail = groups * 8
    sums, powers = [], []
    for g in range(groups):
        s = x[g * 8 : g * 8 + 8]
        powers.append(powers_of(s))
        sums.append(jnp.round(s * units(powers[-1])))
    return jnp.concatenate(sums + powers + [x[tail + groups :]], axis=0)


def decode_sums(x, groups):
    tail = groups * 8
    sums = [x[g * 8 : g * 8 + 8] * scales(x[tail + g : tail + g + 1]) for g in range(groups)]
    return jnp.concatenate(sums + [x[tail:]], axis=0)


def with_rows(tile, rows, groups):
    at = groups * 10
    return jnp.concatenate([tile[:at], *rows, tile[at + len(rows) :]], axis=0)


def block_rows(groups):
    return groups * 8 + -(-2 * groups // 16) * 16


def take_half_kernel(codebook, out, sem):
    _, cols = my_half(out.shape[1])
    copy = pltpu.make_async_copy(codebook.at[:, cols], out, sem)
    copy.start()
    copy.wait()


def begin_kernel(shape, e0, e1, c0, c1, rot, out, codes, rt, v0, lhs, rhs, total):
    rows, half, n_words, n_out = shape
    subs = codes.shape[0]
    core, cols = my_half(half)
    mine = pl.ds(pl.multiple_of(core * subs, 16), subs)
    rot_t = rot[:, cols].T
    for i, (e, c) in enumerate(((e0, c0), (e1, c1))):
        at = slice(i * rows, (i + 1) * rows)
        codes[:, at] = c[mine, :]
        rt[:, at] = lax.dot_general(rot_t, e[...], nt, preferred_element_type=f32).astype(bf16)
    v0[...] = e0[...]
    x = lax.axis_index("replica") // 2
    half_sums(0 if n_out == 1 else 1 - x, n_words, codes, rt, lhs, rhs, total)
    if n_out == 1:
        out[...] = total[...]
        return
    me = lax.axis_index("dp")
    block = total.shape[0] // n_out
    for k in range(n_out):
        at = pl.ds(pl.multiple_of((me ^ k) * block, 16), block)
        out[k * block : (k + 1) * block, :] = encode_sums(total[at, :], subs // pack // 2)


def cross_kernel(shape, e0, e1, codes, first, *rest):
    rows, half, n_words, n_book, n_out = shape
    books, outs, (book, recon, turned, total) = rest[:n_book], rest[n_book:-4], rest[-4:]
    me = lax.axis_index("dp")
    owned = n_words // n_book
    for i, k in enumerate((0,) + hops if n_book > 1 else (0,)):
        book[pl.ds(pl.multiple_of((me ^ k) * owned if n_book > 1 else 0, owned), owned), :] = books[i][...].astype(f32)
    table = book[...].T
    for part in range(half // lane):
        for p in range(part * lane // 16, (part + 1) * lane // 16):
            made = []
            for s in (2 * p, 2 * p + 1):
                parts = []
                for at in range(0, 2 * rows, lane):
                    c = jnp.broadcast_to(codes[s : s + 1, at : at + lane], (8, lane))
                    index = c & (lane - 1)
                    value = None
                    for t in range(0, n_words, lane):
                        found = jnp.take_along_axis(
                            table[s * 8 : s * 8 + 8, t : t + lane], index, axis=1, mode="promise_in_bounds"
                        )
                        value = found if value is None else jnp.where(c >= t, found, value)
                    parts.append(value)
                made.append(jnp.concatenate(parts, axis=1))
            recon[p * 16 : (p + 1) * 16, :] = jnp.concatenate(made, axis=0).astype(bf16)
        cut = slice(part * lane, (part + 1) * lane)
        got = jnp.dot(recon[cut, :rows], e0[...], preferred_element_type=f32)
        turned[cut, :] = got + jnp.dot(recon[cut, rows:], e1[...], preferred_element_type=f32)
    if n_out == 1:
        outs[0][...] = turned[...].T
        outs[1][...] = first[...]
        return
    total[...] = turned[...].T
    own, own_late, message, *sent = outs
    block, sums = total.shape[0] // n_out, first.shape[0] // n_out
    early, late = block // 2, block // 4
    groups = codes.shape[0] // pack // 2
    x = lax.axis_index("replica") // 2
    for k in range(n_out):
        at = (me ^ k) * block
        terms = total[pl.ds(pl.multiple_of(at, 16), early), :]
        if k:
            sent[hops.index(k)][...] = close_early(terms)
        else:
            own[...] = terms
        mine = pl.ds(pl.multiple_of(at + early + x * late, 16), late)
        other = pl.ds(pl.multiple_of(at + early + (1 - x) * late, 16), late)
        own_late[k * late : (k + 1) * late, :] = total[mine, :]
        parts, powers = encode(total[other, :])
        low, high = tiles(first[k * sums : (k + 1) * sums, :])
        size = message.shape[0] // n_out
        message[k * size : (k + 1) * size, :] = whole(
            jnp.concatenate(parts + [with_rows(low, powers, groups), high], axis=0)
        )


def half_sums(part, n_words, codes, rt, lhs, rhs, total):
    width = codes.shape[1]
    coarse = n_words // fine
    shift = fine.bit_length() - 1
    low_mask, coarse_shift = fine - 1, coarse.bit_length() - 1
    groups = codes.shape[0] // pack // 2
    block = block_rows(groups)
    subs = groups * pack
    codes = codes[pl.ds(pl.multiple_of(part * subs, 8), subs), :]
    row8 = lax.broadcasted_iota(i32, (8, width), 0)
    row16 = lax.broadcasted_iota(i32, (16, width), 0)
    steps = [(row16 + 16 * t).astype(f32).astype(bf16) for t in range(fine // 16)]
    one, zero = jnp.ones((16, width), bf16), jnp.zeros((16, width), bf16)
    out_sub = lax.broadcasted_iota(i32, (8, pack * fine), 1) >> shift
    count_row = lax.broadcasted_iota(i32, (16, pack * fine), 0) >> coarse_shift
    count_sub = lax.broadcasted_iota(i32, (16, pack * fine), 1) >> shift
    total[...] = jnp.zeros_like(total)
    for g in range(groups):
        b = g % 2
        high = []
        for s in range(pack):
            code = jnp.broadcast_to(codes[g * pack + s : g * pack + s + 1, :], (8, width))
            high.append(code >> shift)
            low = (code & low_mask).astype(f32)
            low = jnp.concatenate([low, low], axis=0).astype(bf16)
            for t, step in enumerate(steps):
                at = s * fine + t * 16
                rhs[b, at : at + 16, :] = jnp.where(low == step, one, zero)
        for p in range(pack // 2):
            pair = jnp.concatenate([high[2 * p], high[2 * p + 1]], axis=0).astype(f32).astype(bf16)
            r = rt[pl.ds(pl.multiple_of((part * subs + g * pack + 2 * p) * 8, 16), 16), :]
            for h in range(coarse):
                at = h * pack * 8 + p * 16
                lhs[b, at : at + 16, :] = jnp.where(pair == h, r, zero)
        ones = []
        for p in range(pack // 2):
            both = jnp.where(row8 < coarse, high[2 * p], high[2 * p + 1])
            ones.append(jnp.where(both == (row8 & (coarse - 1)), 1.0, 0.0))
        base = coarse * pack * 8
        lhs[b, base : base + 16, :] = jnp.concatenate(ones, axis=0).astype(bf16)
        got = lax.dot_general(lhs[b], rhs[b], nt, preferred_element_type=f32)
        counts = jnp.where(count_row == count_sub, got[base : base + 16], 0.0)
        counts = counts[:8] + counts[8:]
        counts = counts[:coarse] + counts[coarse:]
        for h in range(coarse):
            kept = got[h * 32 : h * 32 + 8]
            for s in range(1, pack):
                kept = jnp.where(out_sub == s, got[h * 32 + s * 8 : h * 32 + s * 8 + 8], kept)
            at = h * block
            total[at + g * 8 : at + g * 8 + 8, :] = kept
            at += groups * 9 + g
            total[at : at + 1, :] = counts[h : h + 1]


def sums_kernel(fixed, codes, rt, _, out, lhs, rhs, total):
    n_words, direct = fixed
    half_sums(lax.axis_index("replica") // 2 if direct else 1, n_words, codes, rt, lhs, rhs, total)
    out[...] = total[...]


def close_early(x):
    parts, powers = encode(x)
    powers.append(jnp.zeros((pad - len(powers), lane), f32))
    return whole(jnp.concatenate(parts + powers, axis=0))


def open_early(x, rows, across):
    at = rows * across
    return decode(x, rows, x[at : at + across])


def open_late(x, rows, across, groups):
    at = rows * across
    low, high = x[at : at + (x.shape[0] - at) // 2], x[at + (x.shape[0] - at) // 2 :]
    powers = low[groups * 10 : groups * 10 + across]
    return decode(x, rows, powers), jnp.concatenate([decode_sums(low, groups), decode_sums(high, groups)], axis=1)


def add_half_kernel(groups, own_late, own_sums, got, *outs):
    me = lax.axis_index("dp")
    n = len(outs)
    late, block, size = own_late.shape[0] // n, own_sums.shape[0] // n, got.shape[0] // n
    across = own_late.shape[1] // lane
    for i, k in enumerate((0,) + hops):
        cross, sums = open_late(got[k * size : (k + 1) * size, :].astype(f32), late, across, groups)
        parts, powers = encode(own_late[k * late : (k + 1) * late, :] + cross)
        sums += own_sums[pl.ds(pl.multiple_of((me ^ k) * block, 16), block), :]
        low, high = tiles(encode_sums(sums, groups))
        outs[i][...] = whole(jnp.concatenate(parts + [with_rows(low, powers, groups), high], axis=0))


def add_early_kernel(own, *rest):
    total = own[...]
    rows = total.shape[0]
    for q in rest[:-1]:
        total += open_early(q[...].astype(f32), rows, total.shape[1] // lane)
    rest[-1][...] = close_early(total)


def add_late_kernel(groups, late, across, *refs):
    cross = sums = None
    for q in refs[:-1]:
        c, s = open_late(q[...].astype(f32), late, across, groups)
        cross, sums = (c, s) if cross is None else (cross + c, sums + s)
    parts, powers = encode(cross)
    low, high = tiles(encode_sums(sums, groups))
    refs[-1][...] = whole(jnp.concatenate(parts + [with_rows(low, powers, groups), high], axis=0))


def finish_kernel(scale, *refs):
    mine, other, (codebook, out, cross, turned) = refs[:4], refs[4:8], refs[8:]
    width = codebook.shape[1]
    half = width // 2
    across = half // lane
    early = cross.shape[0] // 2
    late = early // 2
    core = lax.axis_index("replica") % 2
    low = lax.axis_index("replica") < 2
    groups = half // (8 * pack) // 2
    for start, (a0, a1, b0, b1) in ((core * half, mine), (half - core * half, other)):
        cols = pl.ds(pl.multiple_of(start, lane), half)
        total = open_early(a0[...].astype(f32), early, across) + open_early(a1[...].astype(f32), early, across)
        cross[:early, cols] = total * scale
        lates, halves = zip(*(open_late(b[...].astype(f32), late, across, groups) for b in (b0, b1)))
        for part, (a, b) in enumerate((lates, lates[::-1])):
            cross[early + part * late : early + (part + 1) * late, cols] = jnp.where(low, a, b) * scale
        for part, (a, b) in enumerate((halves, halves[::-1])):
            x = jnp.where(low, a, b)
            for g in range(groups):
                sums = x[g * 8 : g * 8 + 8]
                row = groups * 9 + g
                counts = jnp.broadcast_to(x[row : row + 1], sums.shape)
                for i in range(pack):
                    to = ((part * groups + g) * pack + i) * 8
                    cut = slice(i * fine, (i + 1) * fine)
                    turned[to : to + 8, :] = jnp.concatenate([sums[:, cut], counts[:, cut]], axis=1)
        t = turned[...].T
        old = codebook[:, cols].astype(f32)
        out[:, cols] = (t[:fine] + prior_count * old) / (t[fine:] + prior_count)


def local(embeddings, codes, rotation, codebook):
    rows, width = embeddings.shape
    n_sub = codes.shape[1]
    half = width // 2
    n = lax.axis_size("dp")
    replicas = lax.axis_size("replica")
    n_words = codebook.shape[0] * n
    owned = codebook.shape[0]
    out_rows = width // n
    direct = n == 4 and owned == fine and replicas == 4 and rows * n * replicas < 32768

    def swap(x, bit):
        return lax.ppermute(x, "replica", [(i, i ^ bit) for i in range(replicas)])

    def exchange(blocks):
        return [lax.ppermute(x, "dp", [(i, i ^ k) for i in range(n)]) for k, x in zip(hops, blocks)]

    e1 = swap(embeddings, 1)
    c0 = codes.T
    c1 = swap(c0, 1)
    book = call(
        take_half_kernel,
        jax.ShapeDtypeStruct((owned, half), bf16),
        (codebook,),
        [pltpu.SemaphoreType.DMA(())],
        "take_half",
        flops=1 << 34,
        hbm=(0,),
    )
    if direct:
        books = [book] + exchange([book] * len(hops))
    else:
        books = [lax.all_gather(book, "dp", axis=0, tiled=True)]
    n_out = n if direct else 1
    coarse = n_words // fine
    groups = n_sub // 2 // pack // 2
    block = block_rows(groups)
    lhs_rows = coarse * pack * 8 + 16
    sums_shape = (coarse * block, pack * fine)
    buffers = [
        pltpu.VMEM((2, lhs_rows, 2 * rows), bf16),
        pltpu.VMEM((2, pack * fine, 2 * rows), bf16),
        pltpu.VMEM(sums_shape, f32),
    ]
    first, my_codes, rt, e0 = call(
        lambda *refs: begin_kernel((rows, half, n_words, n_out), *refs),
        [
            jax.ShapeDtypeStruct(sums_shape, f32),
            jax.ShapeDtypeStruct((n_sub // 2, 2 * rows), i32),
            jax.ShapeDtypeStruct((half, 2 * rows), bf16),
            jax.ShapeDtypeStruct(embeddings.shape, bf16),
        ],
        (embeddings, e1, c0, c1, rotation),
        buffers,
        "begin",
        flops=8 * rows * half * width,
    )
    early, late = out_rows // 2, out_rows // 4
    across = half // lane
    late_size = late * across + block * pack * fine // lane
    if direct:
        cross_outs = [
            jax.ShapeDtypeStruct((early, half), f32),
            jax.ShapeDtypeStruct((n * late, half), f32),
            jax.ShapeDtypeStruct((n * late_size, lane), i16),
        ] + [jax.ShapeDtypeStruct((early * across + pad, lane), i16)] * (n - 1)
    else:
        cross_outs = [jax.ShapeDtypeStruct((width, half), f32), jax.ShapeDtypeStruct(first.shape, f32)]
    cross = call(
        lambda *refs: cross_kernel((rows, half, n_words, len(books), n_out), *refs),
        cross_outs,
        (e0, e1, my_codes, first, *books),
        [
            pltpu.VMEM((n_words, half), f32),
            pltpu.VMEM((half, 2 * rows), bf16),
            pltpu.VMEM((half, width), f32),
            pltpu.VMEM((width, half), f32),
        ],
        "cross_terms",
        flops=4 * rows * half * width,
    )
    scale = 1.0 / (rows * n * replicas)
    own = call(
        lambda *refs: sums_kernel((n_words, direct), *refs),
        jax.ShapeDtypeStruct(sums_shape, f32),
        (my_codes, rt, cross[0]),
        buffers,
        "codeword_sums",
        flops=8 * rows * half * width,
        unread=(2,),
    )
    if not direct:
        return plain_finish((cross[1], own), cross[0], codebook, n_words, scale, swap)

    own_early, own_late, message, *early_sent = cross
    late_blocks = call(
        lambda *refs: add_half_kernel(groups, *refs),
        [jax.ShapeDtypeStruct((late_size, lane), i16)] * n,
        (own_late, own, swap(message, 2)),
        [],
        "add_half",
    )
    a = call(
        add_early_kernel,
        jax.ShapeDtypeStruct((early * across + pad, lane), i16),
        (own_early, *exchange(early_sent)),
        [],
        "add_early",
    )
    b = call(
        lambda *refs: add_late_kernel(groups, late, across, *refs),
        jax.ShapeDtypeStruct((late_size, lane), i16),
        (late_blocks[0], *exchange(late_blocks[1:])),
        [],
        "add_late",
    )
    mine = (a, swap(a, 2), b, swap(b, 2))
    return call(
        lambda *refs: finish_kernel(scale, *refs),
        [jax.ShapeDtypeStruct(codebook.shape, f32), jax.ShapeDtypeStruct((out_rows, width), f32)],
        (*mine, *(swap(x, 1) for x in mine), codebook),
        [pltpu.VMEM((half, lane), f32)],
        "finish",
    )


def plain_finish(sums, cross, codebook, n_words, scale, swap):
    half = cross.shape[1]
    coarse = n_words // fine
    groups = half // (8 * pack) // 2
    sums = jnp.stack([x.reshape(coarse, -1, pack * fine) for x in sums])
    counts = sums[:, :, groups * 9 : groups * 10].reshape(2, coarse, groups, pack, fine)
    counts = counts.transpose(1, 4, 0, 2, 3).reshape(n_words, half // 8)
    sums = sums[:, :, : groups * 8].reshape(2, coarse, groups, 8, pack, fine)
    sums = sums.transpose(1, 5, 0, 2, 4, 3).reshape(n_words, half)
    parts = []
    for x in (sums, counts, cross):
        x = lax.psum_scatter(x, "dp", scatter_dimension=0, tiled=True)
        bit = 2
        while bit < lax.axis_size("replica"):
            x = x + swap(x, bit)
            bit *= 2
        y = swap(x, 1)
        first = lax.axis_index("replica") % 2 == 0
        parts.append(jnp.where(first, jnp.concatenate([x, y], 1), jnp.concatenate([y, x], 1)))
    sums, counts, cross = parts
    spread = jnp.repeat(counts, 8, axis=1)
    new_codebook = (sums + prior_count * codebook.astype(f32)) / (spread + prior_count)
    return new_codebook, cross * scale


def solution(mesh):
    in_specs = (
        P(("groups", "dp", "replica"), None),
        P(("groups", "dp", "replica"), None),
        P("groups", None),
        P(("groups", "dp"), None),
    )
    out_specs = (P(("groups", "dp"), None), P(("groups", "dp"), None))
    return jax.shard_map(local, mesh=mesh, in_specs=in_specs, out_specs=out_specs, check_vma=False)
```

```python
import jax
import jax.numpy as jnp
from jax import lax
from jax.experimental import pallas as pl
from jax.experimental.pallas import tpu as pltpu
from jax.sharding import PartitionSpec as P

prior_count = 4.0
lane = 128
book_order, early_order, late_order = (1, 2, 3), (3, 2, 1), (2, 3, 1)
hops = (2, 3, 1)
fine = 64
pack = 4
level = 32000.0
octave = 8.0
pad = 16

f32, bf16, i32, i16 = jnp.float32, jnp.bfloat16, jnp.int32, jnp.int16
nt = (((1,), (1,)), ((), ()))


def call(kernel, outs, args, scratch, name, flops=0, unread=(), hbm=()):
    spaces = [pl.ANY if i in unread + hbm else pltpu.VMEM for i in range(len(args))]
    args = [pltpu.with_memory_space_constraint(x, pltpu.HBM) if i in hbm else x for i, x in enumerate(args)]
    shapes = jax.tree.leaves(outs) + list(args)
    bytes_accessed = sum(s.size * s.dtype.itemsize for s in shapes)
    return pl.pallas_call(
        kernel,
        out_shape=outs,
        in_specs=[pl.BlockSpec(memory_space=space) for space in spaces],
        scratch_shapes=scratch,
        compiler_params=pltpu.CompilerParams(vmem_limit_bytes=20 << 20),
        cost_estimate=pl.CostEstimate(flops=flops, bytes_accessed=bytes_accessed, transcendentals=0),
        name=name,
    )(*args)


def my_half(width):
    core = lax.axis_index("replica") % 2
    return core, pl.ds(pl.multiple_of(core * width, lane), width)


def powers_of(x):
    top = jnp.maximum(jnp.max(jnp.abs(x), axis=0, keepdims=True), 1e-30)
    return jnp.ceil(jnp.log2(top) * octave)


def units(power):
    return level * jnp.exp2(power * (-1.0 / octave))


def scales(power):
    return jnp.exp2(power * (1.0 / octave)) * (1.0 / level)


def tiles(x):
    return [x[:, at : at + lane] for at in range(0, x.shape[1], lane)]


def whole(x):
    return x.astype(i32).astype(i16)


def encode(x):
    power = powers_of(x)
    return tiles(jnp.round(x * units(power))), tiles(power)


def decode(x, rows, powers):
    parts = [x[j * rows : (j + 1) * rows] * scales(powers[j : j + 1]) for j in range(powers.shape[0])]
    return jnp.concatenate(parts, axis=1)


def encode_sums(x, groups):
    tail = groups * 8
    sums, powers = [], []
    for g in range(groups):
        s = x[g * 8 : g * 8 + 8]
        powers.append(powers_of(s))
        sums.append(jnp.round(s * units(powers[-1])))
    return jnp.concatenate(sums + powers + [x[tail + groups :]], axis=0)


def decode_sums(x, groups):
    tail = groups * 8
    sums = [x[g * 8 : g * 8 + 8] * scales(x[tail + g : tail + g + 1]) for g in range(groups)]
    return jnp.concatenate(sums + [x[tail:]], axis=0)


def with_rows(tile, rows, groups):
    at = groups * 10
    return jnp.concatenate([tile[:at], *rows, tile[at + len(rows) :]], axis=0)


def block_rows(groups):
    return groups * 8 + -(-2 * groups // 16) * 16


def take_half_kernel(codebook, out):
    _, cols = my_half(out.shape[1])
    out[...] = codebook[:, cols]


def begin_kernel(shape, e0, e1, c0, c1, rot, out, codes, rt, v0, lhs, rhs, total):
    rows, half, n_words, n_out = shape
    subs = codes.shape[0]
    core, cols = my_half(half)
    mine = pl.ds(pl.multiple_of(core * subs, 16), subs)
    rot_t = rot[:, cols].T
    for i, (e, c) in enumerate(((e0, c0), (e1, c1))):
        at = slice(i * rows, (i + 1) * rows)
        codes[:, at] = c[mine, :]
        rt[:, at] = lax.dot_general(rot_t, e[...], nt, preferred_element_type=f32).astype(bf16)
    v0[...] = e0[...]
    x = lax.axis_index("replica") // 2
    half_sums(0 if n_out == 1 else 1 - x, n_words, codes, rt, lhs, rhs, total)
    if n_out == 1:
        out[...] = total[...]
        return
    me = lax.axis_index("dp")
    block = total.shape[0] // n_out
    for k in range(n_out):
        at = pl.ds(pl.multiple_of((me ^ k) * block, 16), block)
        out[k * block : (k + 1) * block, :] = encode_sums(total[at, :], subs // pack // 2)


def cross_kernel(shape, e0, e1, codes, first, *rest):
    rows, half, n_words, n_book, n_out = shape
    books, outs, (book, recon, turned, total) = rest[:n_book], rest[n_book:-4], rest[-4:]
    me = lax.axis_index("dp")
    owned = n_words // n_book
    for i, k in enumerate((0,) + book_order if n_book > 1 else (0,)):
        book[pl.ds(pl.multiple_of((me ^ k) * owned if n_book > 1 else 0, owned), owned), :] = books[i][...].astype(f32)
    table = book[...].T
    for part in range(half // lane):
        for p in range(part * lane // 16, (part + 1) * lane // 16):
            made = []
            for s in (2 * p, 2 * p + 1):
                parts = []
                for at in range(0, 2 * rows, lane):
                    c = jnp.broadcast_to(codes[s : s + 1, at : at + lane], (8, lane))
                    index = c & (lane - 1)
                    value = None
                    for t in range(0, n_words, lane):
                        found = jnp.take_along_axis(
                            table[s * 8 : s * 8 + 8, t : t + lane], index, axis=1, mode="promise_in_bounds"
                        )
                        value = found if value is None else jnp.where(c >= t, found, value)
                    parts.append(value)
                made.append(jnp.concatenate(parts, axis=1))
            recon[p * 16 : (p + 1) * 16, :] = jnp.concatenate(made, axis=0).astype(bf16)
        cut = slice(part * lane, (part + 1) * lane)
        got = jnp.dot(recon[cut, :rows], e0[...], preferred_element_type=f32)
        turned[cut, :] = got + jnp.dot(recon[cut, rows:], e1[...], preferred_element_type=f32)
    if n_out == 1:
        outs[0][...] = turned[...].T
        outs[1][...] = first[...]
        return
    total[...] = turned[...].T
    own, own_late, message, *sent = outs
    block, sums = total.shape[0] // n_out, first.shape[0] // n_out
    early, late = block // 2, block // 4
    groups = codes.shape[0] // pack // 2
    x = lax.axis_index("replica") // 2
    for k in range(n_out):
        at = (me ^ k) * block
        terms = total[pl.ds(pl.multiple_of(at, 16), early), :]
        if k:
            sent[hops.index(k)][...] = close_early(terms)
        else:
            own[...] = terms
        mine = pl.ds(pl.multiple_of(at + early + x * late, 16), late)
        other = pl.ds(pl.multiple_of(at + early + (1 - x) * late, 16), late)
        own_late[k * late : (k + 1) * late, :] = total[mine, :]
        parts, powers = encode(total[other, :])
        low, high = tiles(first[k * sums : (k + 1) * sums, :])
        size = message.shape[0] // n_out
        message[k * size : (k + 1) * size, :] = whole(
            jnp.concatenate(parts + [with_rows(low, powers, groups), high], axis=0)
        )


def half_sums(part, n_words, codes, rt, lhs, rhs, total):
    width = codes.shape[1]
    coarse = n_words // fine
    shift = fine.bit_length() - 1
    low_mask, coarse_shift = fine - 1, coarse.bit_length() - 1
    groups = codes.shape[0] // pack // 2
    block = block_rows(groups)
    subs = groups * pack
    codes = codes[pl.ds(pl.multiple_of(part * subs, 8), subs), :]
    row8 = lax.broadcasted_iota(i32, (8, width), 0)
    row16 = lax.broadcasted_iota(i32, (16, width), 0)
    steps = [(row16 + 16 * t).astype(f32).astype(bf16) for t in range(fine // 16)]
    one, zero = jnp.ones((16, width), bf16), jnp.zeros((16, width), bf16)
    out_sub = lax.broadcasted_iota(i32, (8, pack * fine), 1) >> shift
    count_row = lax.broadcasted_iota(i32, (16, pack * fine), 0) >> coarse_shift
    count_sub = lax.broadcasted_iota(i32, (16, pack * fine), 1) >> shift
    total[...] = jnp.zeros_like(total)
    for g in range(groups):
        b = g % 2
        high = []
        for s in range(pack):
            code = jnp.broadcast_to(codes[g * pack + s : g * pack + s + 1, :], (8, width))
            high.append(code >> shift)
            low = (code & low_mask).astype(f32)
            low = jnp.concatenate([low, low], axis=0).astype(bf16)
            for t, step in enumerate(steps):
                at = s * fine + t * 16
                rhs[b, at : at + 16, :] = jnp.where(low == step, one, zero)
        for p in range(pack // 2):
            pair = jnp.concatenate([high[2 * p], high[2 * p + 1]], axis=0).astype(f32).astype(bf16)
            r = rt[pl.ds(pl.multiple_of((part * subs + g * pack + 2 * p) * 8, 16), 16), :]
            for h in range(coarse):
                at = h * pack * 8 + p * 16
                lhs[b, at : at + 16, :] = jnp.where(pair == h, r, zero)
        ones = []
        for p in range(pack // 2):
            both = jnp.where(row8 < coarse, high[2 * p], high[2 * p + 1])
            ones.append(jnp.where(both == (row8 & (coarse - 1)), 1.0, 0.0))
        base = coarse * pack * 8
        lhs[b, base : base + 16, :] = jnp.concatenate(ones, axis=0).astype(bf16)
        got = lax.dot_general(lhs[b], rhs[b], nt, preferred_element_type=f32)
        counts = jnp.where(count_row == count_sub, got[base : base + 16], 0.0)
        counts = counts[:8] + counts[8:]
        counts = counts[:coarse] + counts[coarse:]
        for h in range(coarse):
            kept = got[h * 32 : h * 32 + 8]
            for s in range(1, pack):
                kept = jnp.where(out_sub == s, got[h * 32 + s * 8 : h * 32 + s * 8 + 8], kept)
            at = h * block
            total[at + g * 8 : at + g * 8 + 8, :] = kept
            at += groups * 9 + g
            total[at : at + 1, :] = counts[h : h + 1]


def sums_kernel(fixed, codes, rt, _, out, lhs, rhs, total):
    n_words, direct = fixed
    half_sums(lax.axis_index("replica") // 2 if direct else 1, n_words, codes, rt, lhs, rhs, total)
    out[...] = total[...]


def close_early(x):
    parts, powers = encode(x)
    powers.append(jnp.zeros((pad - len(powers), lane), f32))
    return whole(jnp.concatenate(parts + powers, axis=0))


def open_early(x, rows, across):
    at = rows * across
    return decode(x, rows, x[at : at + across])


def open_late(x, rows, across, groups):
    at = rows * across
    low, high = x[at : at + (x.shape[0] - at) // 2], x[at + (x.shape[0] - at) // 2 :]
    powers = low[groups * 10 : groups * 10 + across]
    return decode(x, rows, powers), jnp.concatenate([decode_sums(low, groups), decode_sums(high, groups)], axis=1)


def add_half_kernel(groups, own_late, own_sums, got, *outs):
    me = lax.axis_index("dp")
    n = len(outs)
    late, block, size = own_late.shape[0] // n, own_sums.shape[0] // n, got.shape[0] // n
    across = own_late.shape[1] // lane
    for i, k in enumerate((0,) + hops):
        cross, sums = open_late(got[k * size : (k + 1) * size, :].astype(f32), late, across, groups)
        parts, powers = encode(own_late[k * late : (k + 1) * late, :] + cross)
        sums += own_sums[pl.ds(pl.multiple_of((me ^ k) * block, 16), block), :]
        low, high = tiles(encode_sums(sums, groups))
        outs[i][...] = whole(jnp.concatenate(parts + [with_rows(low, powers, groups), high], axis=0))


def add_early_kernel(own, *rest):
    total = own[...]
    rows = total.shape[0]
    for q in rest[:-1]:
        total += open_early(q[...].astype(f32), rows, total.shape[1] // lane)
    rest[-1][...] = close_early(total)


def add_late_kernel(groups, late, across, *refs):
    cross = sums = None
    for q in refs[:-1]:
        c, s = open_late(q[...].astype(f32), late, across, groups)
        cross, sums = (c, s) if cross is None else (cross + c, sums + s)
    parts, powers = encode(cross)
    low, high = tiles(encode_sums(sums, groups))
    refs[-1][...] = whole(jnp.concatenate(parts + [with_rows(low, powers, groups), high], axis=0))


def finish_kernel(scale, *refs):
    mine, other, (codebook, out, cross, turned) = refs[:4], refs[4:8], refs[8:]
    width = codebook.shape[1]
    half = width // 2
    across = half // lane
    early = cross.shape[0] // 2
    late = early // 2
    core = lax.axis_index("replica") % 2
    low = lax.axis_index("replica") < 2
    groups = half // (8 * pack) // 2
    for start, (a0, a1, b0, b1) in ((core * half, mine), (half - core * half, other)):
        cols = pl.ds(pl.multiple_of(start, lane), half)
        total = open_early(a0[...].astype(f32), early, across) + open_early(a1[...].astype(f32), early, across)
        cross[:early, cols] = total * scale
        lates, halves = zip(*(open_late(b[...].astype(f32), late, across, groups) for b in (b0, b1)))
        for part, (a, b) in enumerate((lates, lates[::-1])):
            cross[early + part * late : early + (part + 1) * late, cols] = jnp.where(low, a, b) * scale
        for part, (a, b) in enumerate((halves, halves[::-1])):
            x = jnp.where(low, a, b)
            for g in range(groups):
                sums = x[g * 8 : g * 8 + 8]
                row = groups * 9 + g
                counts = jnp.broadcast_to(x[row : row + 1], sums.shape)
                for i in range(pack):
                    to = ((part * groups + g) * pack + i) * 8
                    cut = slice(i * fine, (i + 1) * fine)
                    turned[to : to + 8, :] = jnp.concatenate([sums[:, cut], counts[:, cut]], axis=1)
        t = turned[...].T
        old = codebook[:, cols].astype(f32)
        out[:, cols] = (t[:fine] + prior_count * old) / (t[fine:] + prior_count)


def local(embeddings, codes, rotation, codebook):
    rows, width = embeddings.shape
    n_sub = codes.shape[1]
    half = width // 2
    n = lax.axis_size("dp")
    replicas = lax.axis_size("replica")
    n_words = codebook.shape[0] * n
    owned = codebook.shape[0]
    out_rows = width // n
    direct = n == 4 and owned == fine and replicas == 4 and rows * n * replicas < 32768

    def swap(x, bit):
        return lax.ppermute(x, "replica", [(i, i ^ bit) for i in range(replicas)])

    def exchange(blocks, order):
        return [lax.ppermute(blocks[hops.index(k)], "dp", [(i, i ^ k) for i in range(n)]) for k in order]

    e1 = swap(embeddings, 1)
    c0 = codes.T
    c1 = swap(c0, 1)
    book = call(
        take_half_kernel,
        jax.ShapeDtypeStruct((owned, half), bf16),
        (codebook,),
        [],
        "take_half",
        flops=1 << 34,
    )
    if direct:
        books = [book] + exchange([book] * len(hops), book_order)
    else:
        books = [lax.all_gather(book, "dp", axis=0, tiled=True)]
    n_out = n if direct else 1
    coarse = n_words // fine
    groups = n_sub // 2 // pack // 2
    block = block_rows(groups)
    lhs_rows = coarse * pack * 8 + 16
    sums_shape = (coarse * block, pack * fine)
    buffers = [
        pltpu.VMEM((2, lhs_rows, 2 * rows), bf16),
        pltpu.VMEM((2, pack * fine, 2 * rows), bf16),
        pltpu.VMEM(sums_shape, f32),
    ]
    first, my_codes, rt, e0 = call(
        lambda *refs: begin_kernel((rows, half, n_words, n_out), *refs),
        [
            jax.ShapeDtypeStruct(sums_shape, f32),
            jax.ShapeDtypeStruct((n_sub // 2, 2 * rows), i32),
            jax.ShapeDtypeStruct((half, 2 * rows), bf16),
            jax.ShapeDtypeStruct(embeddings.shape, bf16),
        ],
        (embeddings, e1, c0, c1, rotation),
        buffers,
        "begin",
        flops=8 * rows * half * width,
    )
    early, late = out_rows // 2, out_rows // 4
    across = half // lane
    late_size = late * across + block * pack * fine // lane
    if direct:
        cross_outs = [
            jax.ShapeDtypeStruct((early, half), f32),
            jax.ShapeDtypeStruct((n * late, half), f32),
            jax.ShapeDtypeStruct((n * late_size, lane), i16),
        ] + [jax.ShapeDtypeStruct((early * across + pad, lane), i16)] * (n - 1)
    else:
        cross_outs = [jax.ShapeDtypeStruct((width, half), f32), jax.ShapeDtypeStruct(first.shape, f32)]
    cross = call(
        lambda *refs: cross_kernel((rows, half, n_words, len(books), n_out), *refs),
        cross_outs,
        (e0, e1, my_codes, first, *books),
        [
            pltpu.VMEM((n_words, half), f32),
            pltpu.VMEM((half, 2 * rows), bf16),
            pltpu.VMEM((half, width), f32),
            pltpu.VMEM((width, half), f32),
        ],
        "cross_terms",
        flops=4 * rows * half * width,
    )
    scale = 1.0 / (rows * n * replicas)
    own = call(
        lambda *refs: sums_kernel((n_words, direct), *refs),
        jax.ShapeDtypeStruct(sums_shape, f32),
        (my_codes, rt, cross[0]),
        buffers,
        "codeword_sums",
        flops=8 * rows * half * width,
        unread=(2,),
    )
    if not direct:
        return plain_finish((cross[1], own), cross[0], codebook, n_words, scale, swap)

    own_early, own_late, message, *early_sent = cross
    late_blocks = call(
        lambda *refs: add_half_kernel(groups, *refs),
        [jax.ShapeDtypeStruct((late_size, lane), i16)] * n,
        (own_late, own, swap(message, 2)),
        [],
        "add_half",
    )
    a = call(
        add_early_kernel,
        jax.ShapeDtypeStruct((early * across + pad, lane), i16),
        (own_early, *exchange(early_sent, early_order)),
        [],
        "add_early",
    )
    b = call(
        lambda *refs: add_late_kernel(groups, late, across, *refs),
        jax.ShapeDtypeStruct((late_size, lane), i16),
        (late_blocks[0], *exchange(late_blocks[1:], late_order)),
        [],
        "add_late",
    )
    mine = (a, swap(a, 2), b, swap(b, 2))
    return call(
        lambda *refs: finish_kernel(scale, *refs),
        [jax.ShapeDtypeStruct(codebook.shape, f32), jax.ShapeDtypeStruct((out_rows, width), f32)],
        (*mine, *(swap(x, 1) for x in mine), codebook),
        [pltpu.VMEM((half, lane), f32)],
        "finish",
    )


def plain_finish(sums, cross, codebook, n_words, scale, swap):
    half = cross.shape[1]
    coarse = n_words // fine
    groups = half // (8 * pack) // 2
    sums = jnp.stack([x.reshape(coarse, -1, pack * fine) for x in sums])
    counts = sums[:, :, groups * 9 : groups * 10].reshape(2, coarse, groups, pack, fine)
    counts = counts.transpose(1, 4, 0, 2, 3).reshape(n_words, half // 8)
    sums = sums[:, :, : groups * 8].reshape(2, coarse, groups, 8, pack, fine)
    sums = sums.transpose(1, 5, 0, 2, 4, 3).reshape(n_words, half)
    parts = []
    for x in (sums, counts, cross):
        x = lax.psum_scatter(x, "dp", scatter_dimension=0, tiled=True)
        bit = 2
        while bit < lax.axis_size("replica"):
            x = x + swap(x, bit)
            bit *= 2
        y = swap(x, 1)
        first = lax.axis_index("replica") % 2 == 0
        parts.append(jnp.where(first, jnp.concatenate([x, y], 1), jnp.concatenate([y, x], 1)))
    sums, counts, cross = parts
    spread = jnp.repeat(counts, 8, axis=1)
    new_codebook = (sums + prior_count * codebook.astype(f32)) / (spread + prior_count)
    return new_codebook, cross * scale


def solution(mesh):
    in_specs = (
        P(("groups", "dp", "replica"), None),
        P(("groups", "dp", "replica"), None),
        P("groups", None),
        P(("groups", "dp"), None),
    )
    out_specs = (P(("groups", "dp"), None), P(("groups", "dp"), None))
    return jax.shard_map(local, mesh=mesh, in_specs=in_specs, out_specs=out_specs, check_vma=False)
```

```python
import jax
import jax.numpy as jnp
from jax import lax
from jax.experimental import pallas as pl
from jax.experimental.pallas import tpu as pltpu
from jax.sharding import PartitionSpec as P

prior_count = 4.0
lane = 128
book_order, early_order, late_order = (1, 2, 3), (3, 2, 1), (2, 3, 1)
hops = (2, 3, 1)
fine = 64
pack = 4
level = 32000.0
octave = 8.0
pad = 16

f32, bf16, i32, i16 = jnp.float32, jnp.bfloat16, jnp.int32, jnp.int16
nt = (((1,), (1,)), ((), ()))


def call(kernel, outs, args, scratch, name, flops=0, unread=(), hbm=()):
    spaces = [pl.ANY if i in unread + hbm else pltpu.VMEM for i in range(len(args))]
    args = [pltpu.with_memory_space_constraint(x, pltpu.HBM) if i in hbm else x for i, x in enumerate(args)]
    shapes = jax.tree.leaves(outs) + list(args)
    bytes_accessed = sum(s.size * s.dtype.itemsize for s in shapes)
    return pl.pallas_call(
        kernel,
        out_shape=outs,
        in_specs=[pl.BlockSpec(memory_space=space) for space in spaces],
        scratch_shapes=scratch,
        compiler_params=pltpu.CompilerParams(vmem_limit_bytes=20 << 20),
        cost_estimate=pl.CostEstimate(flops=flops, bytes_accessed=bytes_accessed, transcendentals=0),
        name=name,
    )(*args)


def my_half(width):
    core = lax.axis_index("replica") % 2
    return core, pl.ds(pl.multiple_of(core * width, lane), width)


def powers_of(x):
    top = jnp.maximum(jnp.max(jnp.abs(x), axis=0, keepdims=True), 1e-30)
    return jnp.ceil(jnp.log2(top) * octave)


def units(power):
    return level * jnp.exp2(power * (-1.0 / octave))


def scales(power):
    return jnp.exp2(power * (1.0 / octave)) * (1.0 / level)


def tiles(x):
    return [x[:, at : at + lane] for at in range(0, x.shape[1], lane)]


def whole(x):
    return x.astype(i32).astype(i16)


def encode(x):
    power = powers_of(x)
    return tiles(jnp.round(x * units(power))), tiles(power)


def decode(x, rows, powers):
    parts = [x[j * rows : (j + 1) * rows] * scales(powers[j : j + 1]) for j in range(powers.shape[0])]
    return jnp.concatenate(parts, axis=1)


def encode_sums(x, groups):
    tail = groups * 8
    sums, powers = [], []
    for g in range(groups):
        s = x[g * 8 : g * 8 + 8]
        powers.append(powers_of(s))
        sums.append(jnp.round(s * units(powers[-1])))
    return jnp.concatenate(sums + powers + [x[tail + groups :]], axis=0)


def decode_sums(x, groups):
    tail = groups * 8
    sums = [x[g * 8 : g * 8 + 8] * scales(x[tail + g : tail + g + 1]) for g in range(groups)]
    return jnp.concatenate(sums + [x[tail:]], axis=0)


def with_rows(tile, rows, groups):
    at = groups * 10
    return jnp.concatenate([tile[:at], *rows, tile[at + len(rows) :]], axis=0)


def block_rows(groups):
    return groups * 8 + -(-2 * groups // 16) * 16


def take_half_kernel(codebook, out):
    _, cols = my_half(out.shape[1])
    out[...] = codebook[:, cols]


def begin_kernel(shape, e0, e1, c0, c1, rot, out, codes, rt, lhs, rhs, total):
    rows, half, n_words, n_out = shape
    subs = codes.shape[0]
    core, cols = my_half(half)
    mine = pl.ds(pl.multiple_of(core * subs, 16), subs)
    rot_t = rot[:, cols].T
    for i, (e, c) in enumerate(((e0, c0), (e1, c1))):
        at = slice(i * rows, (i + 1) * rows)
        codes[:, at] = c[mine, :]
        rt[:, at] = lax.dot_general(rot_t, e[...], nt, preferred_element_type=f32).astype(bf16)
    x = lax.axis_index("replica") // 2
    half_sums(0 if n_out == 1 else 1 - x, n_words, codes, rt, lhs, rhs, total)
    if n_out == 1:
        out[...] = total[...]
        return
    me = lax.axis_index("dp")
    block = total.shape[0] // n_out
    for k in range(n_out):
        at = pl.ds(pl.multiple_of((me ^ k) * block, 16), block)
        out[k * block : (k + 1) * block, :] = encode_sums(total[at, :], subs // pack // 2)


def cross_kernel(shape, e0, e1, codes, first, *rest):
    rows, half, n_words, n_book, n_out = shape
    books, outs, (book, recon, total) = rest[:n_book], rest[n_book:-3], rest[-3:]
    me = lax.axis_index("dp")
    owned = n_words // n_book
    for i, k in enumerate((0,) + book_order if n_book > 1 else (0,)):
        book[pl.ds(pl.multiple_of((me ^ k) * owned if n_book > 1 else 0, owned), owned), :] = books[i][...].astype(f32)
    table = book[...].T
    for part in range(half // lane):
        for p in range(part * lane // 16, (part + 1) * lane // 16):
            made = []
            for s in (2 * p, 2 * p + 1):
                parts = []
                for at in range(0, 2 * rows, lane):
                    c = jnp.broadcast_to(codes[s : s + 1, at : at + lane], (8, lane))
                    index = c & (lane - 1)
                    value = None
                    for t in range(0, n_words, lane):
                        found = jnp.take_along_axis(
                            table[s * 8 : s * 8 + 8, t : t + lane], index, axis=1, mode="promise_in_bounds"
                        )
                        value = found if value is None else jnp.where(c >= t, found, value)
                    parts.append(value)
                made.append(jnp.concatenate(parts, axis=1))
            recon[p * 16 : (p + 1) * 16, :] = jnp.concatenate(made, axis=0).astype(bf16)
        cut = slice(part * lane, (part + 1) * lane)
        got = jnp.dot(recon[cut, :rows], e0[...], preferred_element_type=f32)
        got += jnp.dot(recon[cut, rows:], e1[...], preferred_element_type=f32)
        total[:, cut] = got.T
    if n_out == 1:
        outs[0][...] = total[...]
        outs[1][...] = first[...]
        return
    own, own_late, message, *sent = outs
    block, sums = total.shape[0] // n_out, first.shape[0] // n_out
    early, late = block // 2, block // 4
    groups = codes.shape[0] // pack // 2
    x = lax.axis_index("replica") // 2
    for k in range(n_out):
        at = (me ^ k) * block
        terms = total[pl.ds(pl.multiple_of(at, 16), early), :]
        if k:
            sent[hops.index(k)][...] = close_early(terms)
        else:
            own[...] = terms
        mine = pl.ds(pl.multiple_of(at + early + x * late, 16), late)
        other = pl.ds(pl.multiple_of(at + early + (1 - x) * late, 16), late)
        own_late[k * late : (k + 1) * late, :] = total[mine, :]
        parts, powers = encode(total[other, :])
        low, high = tiles(first[k * sums : (k + 1) * sums, :])
        size = message.shape[0] // n_out
        message[k * size : (k + 1) * size, :] = whole(
            jnp.concatenate(parts + [with_rows(low, powers, groups), high], axis=0)
        )


def half_sums(part, n_words, codes, rt, lhs, rhs, total):
    width = codes.shape[1]
    coarse = n_words // fine
    shift = fine.bit_length() - 1
    low_mask, coarse_shift = fine - 1, coarse.bit_length() - 1
    groups = codes.shape[0] // pack // 2
    block = block_rows(groups)
    subs = groups * pack
    codes = codes[pl.ds(pl.multiple_of(part * subs, 8), subs), :]
    row8 = lax.broadcasted_iota(i32, (8, width), 0)
    row16 = lax.broadcasted_iota(i32, (16, width), 0)
    steps = [(row16 + 16 * t).astype(f32).astype(bf16) for t in range(fine // 16)]
    one, zero = jnp.ones((16, width), bf16), jnp.zeros((16, width), bf16)
    out_sub = lax.broadcasted_iota(i32, (8, pack * fine), 1) >> shift
    count_row = lax.broadcasted_iota(i32, (16, pack * fine), 0) >> coarse_shift
    count_sub = lax.broadcasted_iota(i32, (16, pack * fine), 1) >> shift
    total[...] = jnp.zeros_like(total)
    for g in range(groups):
        b = g % 2
        high = []
        for s in range(pack):
            code = jnp.broadcast_to(codes[g * pack + s : g * pack + s + 1, :], (8, width))
            high.append(code >> shift)
            low = (code & low_mask).astype(f32)
            low = jnp.concatenate([low, low], axis=0).astype(bf16)
            for t, step in enumerate(steps):
                at = s * fine + t * 16
                rhs[b, at : at + 16, :] = jnp.where(low == step, one, zero)
        for p in range(pack // 2):
            pair = jnp.concatenate([high[2 * p], high[2 * p + 1]], axis=0).astype(f32).astype(bf16)
            r = rt[pl.ds(pl.multiple_of((part * subs + g * pack + 2 * p) * 8, 16), 16), :]
            for h in range(coarse):
                at = h * pack * 8 + p * 16
                lhs[b, at : at + 16, :] = jnp.where(pair == h, r, zero)
        ones = []
        for p in range(pack // 2):
            both = jnp.where(row8 < coarse, high[2 * p], high[2 * p + 1])
            ones.append(jnp.where(both == (row8 & (coarse - 1)), 1.0, 0.0))
        base = coarse * pack * 8
        lhs[b, base : base + 16, :] = jnp.concatenate(ones, axis=0).astype(bf16)
        got = lax.dot_general(rhs[b], lhs[b], nt, preferred_element_type=f32).T
        counts = jnp.where(count_row == count_sub, got[base : base + 16], 0.0)
        counts = counts[:8] + counts[8:]
        counts = counts[:coarse] + counts[coarse:]
        for h in range(coarse):
            kept = got[h * 32 : h * 32 + 8]
            for s in range(1, pack):
                kept = jnp.where(out_sub == s, got[h * 32 + s * 8 : h * 32 + s * 8 + 8], kept)
            at = h * block
            total[at + g * 8 : at + g * 8 + 8, :] = kept
            at += groups * 9 + g
            total[at : at + 1, :] = counts[h : h + 1]


def sums_kernel(fixed, codes, rt, _, out, lhs, rhs, total):
    n_words, direct = fixed
    half_sums(lax.axis_index("replica") // 2 if direct else 1, n_words, codes, rt, lhs, rhs, total)
    out[...] = total[...]


def close_early(x):
    parts, powers = encode(x)
    powers.append(jnp.zeros((pad - len(powers), lane), f32))
    return whole(jnp.concatenate(parts + powers, axis=0))


def open_early(x, rows, across):
    at = rows * across
    return decode(x, rows, x[at : at + across])


def open_late(x, rows, across, groups):
    at = rows * across
    low, high = x[at : at + (x.shape[0] - at) // 2], x[at + (x.shape[0] - at) // 2 :]
    powers = low[groups * 10 : groups * 10 + across]
    return decode(x, rows, powers), jnp.concatenate([decode_sums(low, groups), decode_sums(high, groups)], axis=1)


def add_half_kernel(groups, own_late, own_sums, got, *outs):
    me = lax.axis_index("dp")
    n = len(outs)
    late, block, size = own_late.shape[0] // n, own_sums.shape[0] // n, got.shape[0] // n
    across = own_late.shape[1] // lane
    for i, k in enumerate((0,) + hops):
        cross, sums = open_late(got[k * size : (k + 1) * size, :].astype(f32), late, across, groups)
        parts, powers = encode(own_late[k * late : (k + 1) * late, :] + cross)
        sums += own_sums[pl.ds(pl.multiple_of((me ^ k) * block, 16), block), :]
        low, high = tiles(encode_sums(sums, groups))
        outs[i][...] = whole(jnp.concatenate(parts + [with_rows(low, powers, groups), high], axis=0))


def add_early_kernel(own, *rest):
    total = own[...]
    rows = total.shape[0]
    for q in rest[:-1]:
        total += open_early(q[...].astype(f32), rows, total.shape[1] // lane)
    rest[-1][...] = close_early(total)


def add_late_kernel(groups, late, across, *refs):
    cross = sums = None
    for q in refs[:-1]:
        c, s = open_late(q[...].astype(f32), late, across, groups)
        cross, sums = (c, s) if cross is None else (cross + c, sums + s)
    parts, powers = encode(cross)
    low, high = tiles(encode_sums(sums, groups))
    refs[-1][...] = whole(jnp.concatenate(parts + [with_rows(low, powers, groups), high], axis=0))


def finish_kernel(scale, *refs):
    mine, other, (codebook, out, cross, turned) = refs[:4], refs[4:8], refs[8:]
    width = codebook.shape[1]
    half = width // 2
    across = half // lane
    early = cross.shape[0] // 2
    late = early // 2
    core = lax.axis_index("replica") % 2
    low = lax.axis_index("replica") < 2
    groups = half // (8 * pack) // 2
    for start, (a0, a1, b0, b1) in ((core * half, mine), (half - core * half, other)):
        cols = pl.ds(pl.multiple_of(start, lane), half)
        total = open_early(a0[...].astype(f32), early, across) + open_early(a1[...].astype(f32), early, across)
        cross[:early, cols] = total * scale
        lates, halves = zip(*(open_late(b[...].astype(f32), late, across, groups) for b in (b0, b1)))
        for part, (a, b) in enumerate((lates, lates[::-1])):
            cross[early + part * late : early + (part + 1) * late, cols] = jnp.where(low, a, b) * scale
        for part, (a, b) in enumerate((halves, halves[::-1])):
            x = jnp.where(low, a, b)
            for g in range(groups):
                sums = x[g * 8 : g * 8 + 8]
                row = groups * 9 + g
                counts = jnp.broadcast_to(x[row : row + 1], sums.shape)
                for i in range(pack):
                    to = ((part * groups + g) * pack + i) * 8
                    cut = slice(i * fine, (i + 1) * fine)
                    turned[to : to + 8, :] = jnp.concatenate([sums[:, cut], counts[:, cut]], axis=1)
        t = turned[...].T
        old = codebook[:, cols].astype(f32)
        out[:, cols] = (t[:fine] + prior_count * old) / (t[fine:] + prior_count)


def local(embeddings, codes, rotation, codebook):
    rows, width = embeddings.shape
    n_sub = codes.shape[1]
    half = width // 2
    n = lax.axis_size("dp")
    replicas = lax.axis_size("replica")
    n_words = codebook.shape[0] * n
    owned = codebook.shape[0]
    out_rows = width // n
    direct = n == 4 and owned == fine and replicas == 4 and rows * n * replicas < 32768

    def swap(x, bit):
        return lax.ppermute(x, "replica", [(i, i ^ bit) for i in range(replicas)])

    def exchange(blocks, order):
        return [lax.ppermute(blocks[hops.index(k)], "dp", [(i, i ^ k) for i in range(n)]) for k in order]

    e1 = swap(embeddings, 1)
    c0 = codes.T
    c1 = swap(c0, 1)
    book = call(
        take_half_kernel,
        jax.ShapeDtypeStruct((owned, half), bf16),
        (codebook,),
        [],
        "take_half",
        flops=1 << 34,
    )
    if direct:
        books = [book] + exchange([book] * len(hops), book_order)
    else:
        books = [lax.all_gather(book, "dp", axis=0, tiled=True)]
    n_out = n if direct else 1
    coarse = n_words // fine
    groups = n_sub // 2 // pack // 2
    block = block_rows(groups)
    lhs_rows = coarse * pack * 8 + 16
    sums_shape = (coarse * block, pack * fine)
    buffers = [
        pltpu.VMEM((2, lhs_rows, 2 * rows), bf16),
        pltpu.VMEM((2, pack * fine, 2 * rows), bf16),
        pltpu.VMEM(sums_shape, f32),
    ]
    first, my_codes, rt = call(
        lambda *refs: begin_kernel((rows, half, n_words, n_out), *refs),
        [
            jax.ShapeDtypeStruct(sums_shape, f32),
            jax.ShapeDtypeStruct((n_sub // 2, 2 * rows), i32),
            jax.ShapeDtypeStruct((half, 2 * rows), bf16),
        ],
        (embeddings, e1, c0, c1, rotation),
        buffers,
        "begin",
        flops=8 * rows * half * width,
    )
    early, late = out_rows // 2, out_rows // 4
    across = half // lane
    late_size = late * across + block * pack * fine // lane
    if direct:
        cross_outs = [
            jax.ShapeDtypeStruct((early, half), f32),
            jax.ShapeDtypeStruct((n * late, half), f32),
            jax.ShapeDtypeStruct((n * late_size, lane), i16),
        ] + [jax.ShapeDtypeStruct((early * across + pad, lane), i16)] * (n - 1)
    else:
        cross_outs = [jax.ShapeDtypeStruct((width, half), f32), jax.ShapeDtypeStruct(first.shape, f32)]
    cross = call(
        lambda *refs: cross_kernel((rows, half, n_words, len(books), n_out), *refs),
        cross_outs,
        (embeddings, e1, my_codes, first, *books),
        [
            pltpu.VMEM((n_words, half), f32),
            pltpu.VMEM((half, 2 * rows), bf16),
            pltpu.VMEM((width, half), f32),
        ],
        "cross_terms",
        flops=4 * rows * half * width,
    )
    scale = 1.0 / (rows * n * replicas)
    own = call(
        lambda *refs: sums_kernel((n_words, direct), *refs),
        jax.ShapeDtypeStruct(sums_shape, f32),
        (my_codes, rt, cross[0]),
        buffers,
        "codeword_sums",
        flops=8 * rows * half * width,
        unread=(2,),
    )
    if not direct:
        return plain_finish((cross[1], own), cross[0], codebook, n_words, scale, swap)

    own_early, own_late, message, *early_sent = cross
    late_blocks = call(
        lambda *refs: add_half_kernel(groups, *refs),
        [jax.ShapeDtypeStruct((late_size, lane), i16)] * n,
        (own_late, own, swap(message, 2)),
        [],
        "add_half",
    )
    a = call(
        add_early_kernel,
        jax.ShapeDtypeStruct((early * across + pad, lane), i16),
        (own_early, *exchange(early_sent, early_order)),
        [],
        "add_early",
    )
    b = call(
        lambda *refs: add_late_kernel(groups, late, across, *refs),
        jax.ShapeDtypeStruct((late_size, lane), i16),
        (late_blocks[0], *exchange(late_blocks[1:], late_order)),
        [],
        "add_late",
    )
    mine = (a, swap(a, 2), b, swap(b, 2))
    return call(
        lambda *refs: finish_kernel(scale, *refs),
        [jax.ShapeDtypeStruct(codebook.shape, f32), jax.ShapeDtypeStruct((out_rows, width), f32)],
        (*mine, *(swap(x, 1) for x in mine), codebook),
        [pltpu.VMEM((half, lane), f32)],
        "finish",
    )


def plain_finish(sums, cross, codebook, n_words, scale, swap):
    half = cross.shape[1]
    coarse = n_words // fine
    groups = half // (8 * pack) // 2
    sums = jnp.stack([x.reshape(coarse, -1, pack * fine) for x in sums])
    counts = sums[:, :, groups * 9 : groups * 10].reshape(2, coarse, groups, pack, fine)
    counts = counts.transpose(1, 4, 0, 2, 3).reshape(n_words, half // 8)
    sums = sums[:, :, : groups * 8].reshape(2, coarse, groups, 8, pack, fine)
    sums = sums.transpose(1, 5, 0, 2, 4, 3).reshape(n_words, half)
    parts = []
    for x in (sums, counts, cross):
        x = lax.psum_scatter(x, "dp", scatter_dimension=0, tiled=True)
        bit = 2
        while bit < lax.axis_size("replica"):
            x = x + swap(x, bit)
            bit *= 2
        y = swap(x, 1)
        first = lax.axis_index("replica") % 2 == 0
        parts.append(jnp.where(first, jnp.concatenate([x, y], 1), jnp.concatenate([y, x], 1)))
    sums, counts, cross = parts
    spread = jnp.repeat(counts, 8, axis=1)
    new_codebook = (sums + prior_count * codebook.astype(f32)) / (spread + prior_count)
    return new_codebook, cross * scale


def solution(mesh):
    in_specs = (
        P(("groups", "dp", "replica"), None),
        P(("groups", "dp", "replica"), None),
        P("groups", None),
        P(("groups", "dp"), None),
    )
    out_specs = (P(("groups", "dp"), None), P(("groups", "dp"), None))
    return jax.shard_map(local, mesh=mesh, in_specs=in_specs, out_specs=out_specs, check_vma=False)
```

```python
import jax
import jax.numpy as jnp
from jax import lax
from jax.experimental import pallas as pl
from jax.experimental.pallas import tpu as pltpu
from jax.sharding import PartitionSpec as P

prior_count = 4.0
lane = 128
book_order, early_order, late_order = (1, 2, 3), (3, 2, 1), (2, 3, 1)
hops = (2, 3, 1)
fine = 64
pack = 4
level = 32000.0
octave = 8.0
pad = 16

f32, bf16, i32, i16 = jnp.float32, jnp.bfloat16, jnp.int32, jnp.int16
nt = (((1,), (1,)), ((), ()))


def call(kernel, outs, args, scratch, name, flops=0, unread=(), hbm=()):
    spaces = [pl.ANY if i in unread + hbm else pltpu.VMEM for i in range(len(args))]
    args = [pltpu.with_memory_space_constraint(x, pltpu.HBM) if i in hbm else x for i, x in enumerate(args)]
    shapes = jax.tree.leaves(outs) + list(args)
    bytes_accessed = sum(s.size * s.dtype.itemsize for s in shapes)
    return pl.pallas_call(
        kernel,
        out_shape=outs,
        in_specs=[pl.BlockSpec(memory_space=space) for space in spaces],
        scratch_shapes=scratch,
        compiler_params=pltpu.CompilerParams(vmem_limit_bytes=20 << 20),
        cost_estimate=pl.CostEstimate(flops=flops, bytes_accessed=bytes_accessed, transcendentals=0),
        name=name,
    )(*args)


def my_half(width):
    core = lax.axis_index("replica") % 2
    return core, pl.ds(pl.multiple_of(core * width, lane), width)


def powers_of(x):
    top = jnp.maximum(jnp.max(jnp.abs(x), axis=0, keepdims=True), 1e-30)
    return jnp.ceil(jnp.log2(top) * octave)


def units(power):
    return level * jnp.exp2(power * (-1.0 / octave))


def scales(power):
    return jnp.exp2(power * (1.0 / octave)) * (1.0 / level)


def tiles(x):
    return [x[:, at : at + lane] for at in range(0, x.shape[1], lane)]


def whole(x):
    return x.astype(i32).astype(i16)


def encode(x):
    power = powers_of(x)
    return tiles(jnp.round(x * units(power))), tiles(power)


def decode(x, rows, powers):
    parts = [x[j * rows : (j + 1) * rows] * scales(powers[j : j + 1]) for j in range(powers.shape[0])]
    return jnp.concatenate(parts, axis=1)


def encode_sums(x, groups):
    tail = groups * 8
    sums, powers = [], []
    for g in range(groups):
        s = x[g * 8 : g * 8 + 8]
        powers.append(powers_of(s))
        sums.append(jnp.round(s * units(powers[-1])))
    return jnp.concatenate(sums + powers + [x[tail + groups :]], axis=0)


def decode_sums(x, groups):
    tail = groups * 8
    sums = [x[g * 8 : g * 8 + 8] * scales(x[tail + g : tail + g + 1]) for g in range(groups)]
    return jnp.concatenate(sums + [x[tail:]], axis=0)


def with_rows(tile, rows, groups):
    at = groups * 10
    return jnp.concatenate([tile[:at], *rows, tile[at + len(rows) :]], axis=0)


def block_rows(groups):
    return groups * 8 + -(-2 * groups // 16) * 16


def blank_kernel(out):
    out[...] = jnp.zeros_like(out)


def take_half_kernel(codebook, _, out):
    _, cols = my_half(out.shape[1])
    out[...] = codebook[:, cols]


def begin_kernel(shape, e0, e1, c0, c1, rot, out, codes, rt, lhs, rhs, total):
    rows, half, n_words, n_out = shape
    subs = codes.shape[0]
    core, cols = my_half(half)
    mine = pl.ds(pl.multiple_of(core * subs, 16), subs)
    rot_t = rot[:, cols].T
    for i, (e, c) in enumerate(((e0, c0), (e1, c1))):
        at = slice(i * rows, (i + 1) * rows)
        codes[:, at] = c[mine, :]
        rt[:, at] = lax.dot_general(rot_t, e[...], nt, preferred_element_type=f32).astype(bf16)
    x = lax.axis_index("replica") // 2
    half_sums(0 if n_out == 1 else 1 - x, n_words, codes, rt, lhs, rhs, total)
    if n_out == 1:
        out[...] = total[...]
        return
    me = lax.axis_index("dp")
    block = total.shape[0] // n_out
    for k in range(n_out):
        at = pl.ds(pl.multiple_of((me ^ k) * block, 16), block)
        out[k * block : (k + 1) * block, :] = encode_sums(total[at, :], subs // pack // 2)


def cross_kernel(shape, e0, e1, codes, first, *rest):
    rows, half, n_words, n_book, n_out = shape
    books, outs, (book, recon, total) = rest[:n_book], rest[n_book:-3], rest[-3:]
    me = lax.axis_index("dp")
    owned = n_words // n_book
    for i, k in enumerate((0,) + book_order if n_book > 1 else (0,)):
        book[pl.ds(pl.multiple_of((me ^ k) * owned if n_book > 1 else 0, owned), owned), :] = books[i][...].astype(f32)
    table = book[...].T
    for part in range(half // lane):
        for p in range(part * lane // 16, (part + 1) * lane // 16):
            made = []
            for s in (2 * p, 2 * p + 1):
                parts = []
                for at in range(0, 2 * rows, lane):
                    c = jnp.broadcast_to(codes[s : s + 1, at : at + lane], (8, lane))
                    index = c & (lane - 1)
                    value = None
                    for t in range(0, n_words, lane):
                        found = jnp.take_along_axis(
                            table[s * 8 : s * 8 + 8, t : t + lane], index, axis=1, mode="promise_in_bounds"
                        )
                        value = found if value is None else jnp.where(c >= t, found, value)
                    parts.append(value)
                made.append(jnp.concatenate(parts, axis=1))
            recon[p * 16 : (p + 1) * 16, :] = jnp.concatenate(made, axis=0).astype(bf16)
        cut = slice(part * lane, (part + 1) * lane)
        got = jnp.dot(recon[cut, :rows], e0[...], preferred_element_type=f32)
        got += jnp.dot(recon[cut, rows:], e1[...], preferred_element_type=f32)
        total[:, cut] = got.T
    if n_out == 1:
        outs[0][...] = total[...]
        outs[1][...] = first[...]
        return
    own, own_late, message, *sent = outs
    block, sums = total.shape[0] // n_out, first.shape[0] // n_out
    early, late = block // 2, block // 4
    groups = codes.shape[0] // pack // 2
    x = lax.axis_index("replica") // 2
    for k in range(n_out):
        at = (me ^ k) * block
        terms = total[pl.ds(pl.multiple_of(at, 16), early), :]
        if k:
            sent[hops.index(k)][...] = close_early(terms)
        else:
            own[...] = terms
        mine = pl.ds(pl.multiple_of(at + early + x * late, 16), late)
        other = pl.ds(pl.multiple_of(at + early + (1 - x) * late, 16), late)
        own_late[k * late : (k + 1) * late, :] = total[mine, :]
        parts, powers = encode(total[other, :])
        low, high = tiles(first[k * sums : (k + 1) * sums, :])
        size = message.shape[0] // n_out
        message[k * size : (k + 1) * size, :] = whole(
            jnp.concatenate(parts + [with_rows(low, powers, groups), high], axis=0)
        )


def half_sums(part, n_words, codes, rt, lhs, rhs, total):
    width = codes.shape[1]
    coarse = n_words // fine
    shift = fine.bit_length() - 1
    low_mask, coarse_shift = fine - 1, coarse.bit_length() - 1
    groups = codes.shape[0] // pack // 2
    block = block_rows(groups)
    subs = groups * pack
    codes = codes[pl.ds(pl.multiple_of(part * subs, 8), subs), :]
    row8 = lax.broadcasted_iota(i32, (8, width), 0)
    row16 = lax.broadcasted_iota(i32, (16, width), 0)
    steps = [(row16 + 16 * t).astype(f32).astype(bf16) for t in range(fine // 16)]
    one, zero = jnp.ones((16, width), bf16), jnp.zeros((16, width), bf16)
    out_sub = lax.broadcasted_iota(i32, (8, pack * fine), 1) >> shift
    count_row = lax.broadcasted_iota(i32, (16, pack * fine), 0) >> coarse_shift
    count_sub = lax.broadcasted_iota(i32, (16, pack * fine), 1) >> shift
    total[...] = jnp.zeros_like(total)
    for g in range(groups):
        b = g % 2
        high = []
        for s in range(pack):
            code = jnp.broadcast_to(codes[g * pack + s : g * pack + s + 1, :], (8, width))
            high.append(code >> shift)
            low = (code & low_mask).astype(f32)
            low = jnp.concatenate([low, low], axis=0).astype(bf16)
            for t, step in enumerate(steps):
                at = s * fine + t * 16
                rhs[b, at : at + 16, :] = jnp.where(low == step, one, zero)
        for p in range(pack // 2):
            pair = jnp.concatenate([high[2 * p], high[2 * p + 1]], axis=0).astype(f32).astype(bf16)
            r = rt[pl.ds(pl.multiple_of((part * subs + g * pack + 2 * p) * 8, 16), 16), :]
            for h in range(coarse):
                at = h * pack * 8 + p * 16
                lhs[b, at : at + 16, :] = jnp.where(pair == h, r, zero)
        ones = []
        for p in range(pack // 2):
            both = jnp.where(row8 < coarse, high[2 * p], high[2 * p + 1])
            ones.append(jnp.where(both == (row8 & (coarse - 1)), 1.0, 0.0))
        base = coarse * pack * 8
        lhs[b, base : base + 16, :] = jnp.concatenate(ones, axis=0).astype(bf16)
        got = lax.dot_general(rhs[b], lhs[b], nt, preferred_element_type=f32).T
        counts = jnp.where(count_row == count_sub, got[base : base + 16], 0.0)
        counts = counts[:8] + counts[8:]
        counts = counts[:coarse] + counts[coarse:]
        for h in range(coarse):
            kept = got[h * 32 : h * 32 + 8]
            for s in range(1, pack):
                kept = jnp.where(out_sub == s, got[h * 32 + s * 8 : h * 32 + s * 8 + 8], kept)
            at = h * block
            total[at + g * 8 : at + g * 8 + 8, :] = kept
            at += groups * 9 + g
            total[at : at + 1, :] = counts[h : h + 1]


def sums_kernel(fixed, codes, rt, _, out, lhs, rhs, total):
    n_words, direct = fixed
    half_sums(lax.axis_index("replica") // 2 if direct else 1, n_words, codes, rt, lhs, rhs, total)
    out[...] = total[...]


def close_early(x):
    parts, powers = encode(x)
    powers.append(jnp.zeros((pad - len(powers), lane), f32))
    return whole(jnp.concatenate(parts + powers, axis=0))


def open_early(x, rows, across):
    at = rows * across
    return decode(x, rows, x[at : at + across])


def open_late(x, rows, across, groups):
    at = rows * across
    low, high = x[at : at + (x.shape[0] - at) // 2], x[at + (x.shape[0] - at) // 2 :]
    powers = low[groups * 10 : groups * 10 + across]
    return decode(x, rows, powers), jnp.concatenate([decode_sums(low, groups), decode_sums(high, groups)], axis=1)


def add_half_kernel(groups, own_late, own_sums, got, *outs):
    me = lax.axis_index("dp")
    n = len(outs)
    late, block, size = own_late.shape[0] // n, own_sums.shape[0] // n, got.shape[0] // n
    across = own_late.shape[1] // lane
    for i, k in enumerate((0,) + hops):
        cross, sums = open_late(got[k * size : (k + 1) * size, :].astype(f32), late, across, groups)
        parts, powers = encode(own_late[k * late : (k + 1) * late, :] + cross)
        sums += own_sums[pl.ds(pl.multiple_of((me ^ k) * block, 16), block), :]
        low, high = tiles(encode_sums(sums, groups))
        outs[i][...] = whole(jnp.concatenate(parts + [with_rows(low, powers, groups), high], axis=0))


def add_early_kernel(own, *rest):
    total = own[...]
    rows = total.shape[0]
    for q in rest[:-1]:
        total += open_early(q[...].astype(f32), rows, total.shape[1] // lane)
    rest[-1][...] = close_early(total)


def add_late_kernel(groups, late, across, *refs):
    cross = sums = None
    for q in refs[:-1]:
        c, s = open_late(q[...].astype(f32), late, across, groups)
        cross, sums = (c, s) if cross is None else (cross + c, sums + s)
    parts, powers = encode(cross)
    low, high = tiles(encode_sums(sums, groups))
    refs[-1][...] = whole(jnp.concatenate(parts + [with_rows(low, powers, groups), high], axis=0))


def finish_kernel(scale, *refs):
    mine, other, (codebook, out, cross, turned) = refs[:4], refs[4:8], refs[8:]
    width = codebook.shape[1]
    half = width // 2
    across = half // lane
    early = cross.shape[0] // 2
    late = early // 2
    core = lax.axis_index("replica") % 2
    low = lax.axis_index("replica") < 2
    groups = half // (8 * pack) // 2
    for start, (a0, a1, b0, b1) in ((core * half, mine), (half - core * half, other)):
        cols = pl.ds(pl.multiple_of(start, lane), half)
        total = open_early(a0[...].astype(f32), early, across) + open_early(a1[...].astype(f32), early, across)
        cross[:early, cols] = total * scale
        lates, halves = zip(*(open_late(b[...].astype(f32), late, across, groups) for b in (b0, b1)))
        for part, (a, b) in enumerate((lates, lates[::-1])):
            cross[early + part * late : early + (part + 1) * late, cols] = jnp.where(low, a, b) * scale
        for part, (a, b) in enumerate((halves, halves[::-1])):
            x = jnp.where(low, a, b)
            for g in range(groups):
                sums = x[g * 8 : g * 8 + 8]
                row = groups * 9 + g
                counts = jnp.broadcast_to(x[row : row + 1], sums.shape)
                for i in range(pack):
                    to = ((part * groups + g) * pack + i) * 8
                    cut = slice(i * fine, (i + 1) * fine)
                    turned[to : to + 8, :] = jnp.concatenate([sums[:, cut], counts[:, cut]], axis=1)
        t = turned[...].T
        old = codebook[:, cols].astype(f32)
        out[:, cols] = (t[:fine] + prior_count * old) / (t[fine:] + prior_count)


def local(embeddings, codes, rotation, codebook):
    rows, width = embeddings.shape
    n_sub = codes.shape[1]
    half = width // 2
    n = lax.axis_size("dp")
    replicas = lax.axis_size("replica")
    n_words = codebook.shape[0] * n
    owned = codebook.shape[0]
    out_rows = width // n
    direct = n == 4 and owned == fine and replicas == 4 and rows * n * replicas < 32768

    def swap(x, bit):
        return lax.ppermute(x, "replica", [(i, i ^ bit) for i in range(replicas)])

    def exchange(blocks, order):
        return [lax.ppermute(blocks[hops.index(k)], "dp", [(i, i ^ k) for i in range(n)]) for k in order]

    e1 = swap(embeddings, 1)
    c0 = codes.T
    c1 = swap(c0, 1)
    blank = call(blank_kernel, jax.ShapeDtypeStruct((8, lane), f32), (), [], "blank", flops=1 << 34)
    book = call(
        take_half_kernel,
        jax.ShapeDtypeStruct((owned, half), bf16),
        (codebook, blank),
        [],
        "take_half",
        flops=1 << 34,
        unread=(1,),
    )
    if direct:
        books = [book] + exchange([book] * len(hops), book_order)
    else:
        books = [lax.all_gather(book, "dp", axis=0, tiled=True)]
    n_out = n if direct else 1
    coarse = n_words // fine
    groups = n_sub // 2 // pack // 2
    block = block_rows(groups)
    lhs_rows = coarse * pack * 8 + 16
    sums_shape = (coarse * block, pack * fine)
    buffers = [
        pltpu.VMEM((2, lhs_rows, 2 * rows), bf16),
        pltpu.VMEM((2, pack * fine, 2 * rows), bf16),
        pltpu.VMEM(sums_shape, f32),
    ]
    first, my_codes, rt = call(
        lambda *refs: begin_kernel((rows, half, n_words, n_out), *refs),
        [
            jax.ShapeDtypeStruct(sums_shape, f32),
            jax.ShapeDtypeStruct((n_sub // 2, 2 * rows), i32),
            jax.ShapeDtypeStruct((half, 2 * rows), bf16),
        ],
        (embeddings, e1, c0, c1, rotation),
        buffers,
        "begin",
        flops=8 * rows * half * width,
    )
    early, late = out_rows // 2, out_rows // 4
    across = half // lane
    late_size = late * across + block * pack * fine // lane
    if direct:
        cross_outs = [
            jax.ShapeDtypeStruct((early, half), f32),
            jax.ShapeDtypeStruct((n * late, half), f32),
            jax.ShapeDtypeStruct((n * late_size, lane), i16),
        ] + [jax.ShapeDtypeStruct((early * across + pad, lane), i16)] * (n - 1)
    else:
        cross_outs = [jax.ShapeDtypeStruct((width, half), f32), jax.ShapeDtypeStruct(first.shape, f32)]
    cross = call(
        lambda *refs: cross_kernel((rows, half, n_words, len(books), n_out), *refs),
        cross_outs,
        (embeddings, e1, my_codes, first, *books),
        [
            pltpu.VMEM((n_words, half), f32),
            pltpu.VMEM((half, 2 * rows), bf16),
            pltpu.VMEM((width, half), f32),
        ],
        "cross_terms",
        flops=4 * rows * half * width,
    )
    scale = 1.0 / (rows * n * replicas)
    own = call(
        lambda *refs: sums_kernel((n_words, direct), *refs),
        jax.ShapeDtypeStruct(sums_shape, f32),
        (my_codes, rt, cross[0]),
        buffers,
        "codeword_sums",
        flops=8 * rows * half * width,
        unread=(2,),
    )
    if not direct:
        return plain_finish((cross[1], own), cross[0], codebook, n_words, scale, swap)

    own_early, own_late, message, *early_sent = cross
    late_blocks = call(
        lambda *refs: add_half_kernel(groups, *refs),
        [jax.ShapeDtypeStruct((late_size, lane), i16)] * n,
        (own_late, own, swap(message, 2)),
        [],
        "add_half",
    )
    a = call(
        add_early_kernel,
        jax.ShapeDtypeStruct((early * across + pad, lane), i16),
        (own_early, *exchange(early_sent, early_order)),
        [],
        "add_early",
    )
    b = call(
        lambda *refs: add_late_kernel(groups, late, across, *refs),
        jax.ShapeDtypeStruct((late_size, lane), i16),
        (late_blocks[0], *exchange(late_blocks[1:], late_order)),
        [],
        "add_late",
    )
    mine = (a, swap(a, 2), b, swap(b, 2))
    return call(
        lambda *refs: finish_kernel(scale, *refs),
        [jax.ShapeDtypeStruct(codebook.shape, f32), jax.ShapeDtypeStruct((out_rows, width), f32)],
        (*mine, *(swap(x, 1) for x in mine), codebook),
        [pltpu.VMEM((half, lane), f32)],
        "finish",
    )


def plain_finish(sums, cross, codebook, n_words, scale, swap):
    half = cross.shape[1]
    coarse = n_words // fine
    groups = half // (8 * pack) // 2
    sums = jnp.stack([x.reshape(coarse, -1, pack * fine) for x in sums])
    counts = sums[:, :, groups * 9 : groups * 10].reshape(2, coarse, groups, pack, fine)
    counts = counts.transpose(1, 4, 0, 2, 3).reshape(n_words, half // 8)
    sums = sums[:, :, : groups * 8].reshape(2, coarse, groups, 8, pack, fine)
    sums = sums.transpose(1, 5, 0, 2, 4, 3).reshape(n_words, half)
    parts = []
    for x in (sums, counts, cross):
        x = lax.psum_scatter(x, "dp", scatter_dimension=0, tiled=True)
        bit = 2
        while bit < lax.axis_size("replica"):
            x = x + swap(x, bit)
            bit *= 2
        y = swap(x, 1)
        first = lax.axis_index("replica") % 2 == 0
        parts.append(jnp.where(first, jnp.concatenate([x, y], 1), jnp.concatenate([y, x], 1)))
    sums, counts, cross = parts
    spread = jnp.repeat(counts, 8, axis=1)
    new_codebook = (sums + prior_count * codebook.astype(f32)) / (spread + prior_count)
    return new_codebook, cross * scale


def solution(mesh):
    in_specs = (
        P(("groups", "dp", "replica"), None),
        P(("groups", "dp", "replica"), None),
        P("groups", None),
        P(("groups", "dp"), None),
    )
    out_specs = (P(("groups", "dp"), None), P(("groups", "dp"), None))
    return jax.shard_map(local, mesh=mesh, in_specs=in_specs, out_specs=out_specs, check_vma=False)
```

```python
import jax
import jax.numpy as jnp
from jax import lax
from jax.experimental import pallas as pl
from jax.experimental.pallas import tpu as pltpu
from jax.sharding import PartitionSpec as P

prior_count = 4.0
lane = 128
book_order, early_order, late_order = (1, 2, 3), (3, 2, 1), (2, 3, 1)
hops = (2, 3, 1)
fine = 64
pack = 4
level = 32000.0
octave = 8.0
pad = 16

f32, bf16, i32, i16 = jnp.float32, jnp.bfloat16, jnp.int32, jnp.int16
nt = (((1,), (1,)), ((), ()))


def call(kernel, outs, args, scratch, name, flops=0, unread=(), hbm=()):
    spaces = [pl.ANY if i in unread + hbm else pltpu.VMEM for i in range(len(args))]
    args = [pltpu.with_memory_space_constraint(x, pltpu.HBM) if i in hbm else x for i, x in enumerate(args)]
    shapes = jax.tree.leaves(outs) + list(args)
    bytes_accessed = sum(s.size * s.dtype.itemsize for s in shapes)
    return pl.pallas_call(
        kernel,
        out_shape=outs,
        in_specs=[pl.BlockSpec(memory_space=space) for space in spaces],
        scratch_shapes=scratch,
        compiler_params=pltpu.CompilerParams(vmem_limit_bytes=20 << 20),
        cost_estimate=pl.CostEstimate(flops=flops, bytes_accessed=bytes_accessed, transcendentals=0),
        name=name,
    )(*args)


def my_half(width):
    core = lax.axis_index("replica") % 2
    return core, pl.ds(pl.multiple_of(core * width, lane), width)


def powers_of(x):
    top = jnp.maximum(jnp.max(jnp.abs(x), axis=0, keepdims=True), 1e-30)
    return jnp.ceil(jnp.log2(top) * octave)


def units(power):
    return level * jnp.exp2(power * (-1.0 / octave))


def scales(power):
    return jnp.exp2(power * (1.0 / octave)) * (1.0 / level)


def tiles(x):
    return [x[:, at : at + lane] for at in range(0, x.shape[1], lane)]


def whole(x):
    return x.astype(i32).astype(i16)


def encode(x):
    power = powers_of(x)
    return tiles(jnp.round(x * units(power))), tiles(power)


def decode(x, rows, powers):
    parts = [x[j * rows : (j + 1) * rows] * scales(powers[j : j + 1]) for j in range(powers.shape[0])]
    return jnp.concatenate(parts, axis=1)


def encode_sums(x, groups):
    tail = groups * 8
    sums, powers = [], []
    for g in range(groups):
        s = x[g * 8 : g * 8 + 8]
        powers.append(powers_of(s))
        sums.append(jnp.round(s * units(powers[-1])))
    return jnp.concatenate(sums + powers + [x[tail + groups :]], axis=0)


def decode_sums(x, groups):
    tail = groups * 8
    sums = [x[g * 8 : g * 8 + 8] * scales(x[tail + g : tail + g + 1]) for g in range(groups)]
    return jnp.concatenate(sums + [x[tail:]], axis=0)


def with_rows(tile, rows, groups):
    at = groups * 10
    return jnp.concatenate([tile[:at], *rows, tile[at + len(rows) :]], axis=0)


def block_rows(groups):
    return groups * 8 + -(-2 * groups // 16) * 16


def blank_kernel(out):
    out[...] = jnp.zeros_like(out)


def take_half_kernel(codebook, _, out):
    _, cols = my_half(out.shape[1])
    out[...] = codebook[:, cols]


def begin_kernel(shape, c0, c1, e0, e1, rot, out, codes, rt, lhs, rhs, total):
    rows, half, n_words, n_out = shape
    subs = codes.shape[0]
    core, cols = my_half(half)
    mine = pl.ds(pl.multiple_of(core * subs, 16), subs)
    rot_t = rot[:, cols].T
    for i, (e, c) in enumerate(((e0, c0), (e1, c1))):
        at = slice(i * rows, (i + 1) * rows)
        codes[:, at] = c[mine, :]
        rt[:, at] = lax.dot_general(rot_t, e[...], nt, preferred_element_type=f32).astype(bf16)
    x = lax.axis_index("replica") // 2
    half_sums(0 if n_out == 1 else 1 - x, n_words, codes, rt, lhs, rhs, total)
    if n_out == 1:
        out[...] = total[...]
        return
    me = lax.axis_index("dp")
    block = total.shape[0] // n_out
    for k in range(n_out):
        at = pl.ds(pl.multiple_of((me ^ k) * block, 16), block)
        out[k * block : (k + 1) * block, :] = encode_sums(total[at, :], subs // pack // 2)


def cross_kernel(shape, e0, e1, codes, first, *rest):
    rows, half, n_words, n_book, n_out = shape
    books, outs, (book, recon, total) = rest[:n_book], rest[n_book:-3], rest[-3:]
    me = lax.axis_index("dp")
    owned = n_words // n_book
    for i, k in enumerate((0,) + book_order if n_book > 1 else (0,)):
        book[pl.ds(pl.multiple_of((me ^ k) * owned if n_book > 1 else 0, owned), owned), :] = books[i][...].astype(f32)
    table = book[...].T
    for part in range(half // lane):
        for p in range(part * lane // 16, (part + 1) * lane // 16):
            made = []
            for s in (2 * p, 2 * p + 1):
                parts = []
                for at in range(0, 2 * rows, lane):
                    c = jnp.broadcast_to(codes[s : s + 1, at : at + lane], (8, lane))
                    index = c & (lane - 1)
                    value = None
                    for t in range(0, n_words, lane):
                        found = jnp.take_along_axis(
                            table[s * 8 : s * 8 + 8, t : t + lane], index, axis=1, mode="promise_in_bounds"
                        )
                        value = found if value is None else jnp.where(c >= t, found, value)
                    parts.append(value)
                made.append(jnp.concatenate(parts, axis=1))
            recon[p * 16 : (p + 1) * 16, :] = jnp.concatenate(made, axis=0).astype(bf16)
        cut = slice(part * lane, (part + 1) * lane)
        got = jnp.dot(recon[cut, :rows], e0[...], preferred_element_type=f32)
        got += jnp.dot(recon[cut, rows:], e1[...], preferred_element_type=f32)
        total[:, cut] = got.T
    if n_out == 1:
        outs[0][...] = total[...]
        outs[1][...] = first[...]
        return
    own, own_late, message, *sent = outs
    block, sums = total.shape[0] // n_out, first.shape[0] // n_out
    early, late = block // 2, block // 4
    groups = codes.shape[0] // pack // 2
    x = lax.axis_index("replica") // 2
    for k in range(n_out):
        at = (me ^ k) * block
        terms = total[pl.ds(pl.multiple_of(at, 16), early), :]
        if k:
            sent[hops.index(k)][...] = close_early(terms)
        else:
            own[...] = terms
        mine = pl.ds(pl.multiple_of(at + early + x * late, 16), late)
        other = pl.ds(pl.multiple_of(at + early + (1 - x) * late, 16), late)
        own_late[k * late : (k + 1) * late, :] = total[mine, :]
        parts, powers = encode(total[other, :])
        low, high = tiles(first[k * sums : (k + 1) * sums, :])
        size = message.shape[0] // n_out
        message[k * size : (k + 1) * size, :] = whole(
            jnp.concatenate(parts + [with_rows(low, powers, groups), high], axis=0)
        )


def half_sums(part, n_words, codes, rt, lhs, rhs, total):
    width = codes.shape[1]
    coarse = n_words // fine
    shift = fine.bit_length() - 1
    low_mask, coarse_shift = fine - 1, coarse.bit_length() - 1
    groups = codes.shape[0] // pack // 2
    block = block_rows(groups)
    subs = groups * pack
    codes = codes[pl.ds(pl.multiple_of(part * subs, 8), subs), :]
    row8 = lax.broadcasted_iota(i32, (8, width), 0)
    row16 = lax.broadcasted_iota(i32, (16, width), 0)
    steps = [(row16 + 16 * t).astype(f32).astype(bf16) for t in range(fine // 16)]
    one, zero = jnp.ones((16, width), bf16), jnp.zeros((16, width), bf16)
    out_sub = lax.broadcasted_iota(i32, (8, pack * fine), 1) >> shift
    count_row = lax.broadcasted_iota(i32, (16, pack * fine), 0) >> coarse_shift
    count_sub = lax.broadcasted_iota(i32, (16, pack * fine), 1) >> shift
    total[...] = jnp.zeros_like(total)
    for g in range(groups):
        b = g % 2
        high = []
        for s in range(pack):
            code = jnp.broadcast_to(codes[g * pack + s : g * pack + s + 1, :], (8, width))
            high.append(code >> shift)
            low = (code & low_mask).astype(f32)
            low = jnp.concatenate([low, low], axis=0).astype(bf16)
            for t, step in enumerate(steps):
                at = s * fine + t * 16
                rhs[b, at : at + 16, :] = jnp.where(low == step, one, zero)
        for p in range(pack // 2):
            pair = jnp.concatenate([high[2 * p], high[2 * p + 1]], axis=0).astype(f32).astype(bf16)
            r = rt[pl.ds(pl.multiple_of((part * subs + g * pack + 2 * p) * 8, 16), 16), :]
            for h in range(coarse):
                at = h * pack * 8 + p * 16
                lhs[b, at : at + 16, :] = jnp.where(pair == h, r, zero)
        ones = []
        for p in range(pack // 2):
            both = jnp.where(row8 < coarse, high[2 * p], high[2 * p + 1])
            ones.append(jnp.where(both == (row8 & (coarse - 1)), 1.0, 0.0))
        base = coarse * pack * 8
        lhs[b, base : base + 16, :] = jnp.concatenate(ones, axis=0).astype(bf16)
        got = lax.dot_general(rhs[b], lhs[b], nt, preferred_element_type=f32).T
        counts = jnp.where(count_row == count_sub, got[base : base + 16], 0.0)
        counts = counts[:8] + counts[8:]
        counts = counts[:coarse] + counts[coarse:]
        for h in range(coarse):
            kept = got[h * 32 : h * 32 + 8]
            for s in range(1, pack):
                kept = jnp.where(out_sub == s, got[h * 32 + s * 8 : h * 32 + s * 8 + 8], kept)
            at = h * block
            total[at + g * 8 : at + g * 8 + 8, :] = kept
            at += groups * 9 + g
            total[at : at + 1, :] = counts[h : h + 1]


def sums_kernel(fixed, codes, rt, _, out, lhs, rhs, total):
    n_words, direct = fixed
    half_sums(lax.axis_index("replica") // 2 if direct else 1, n_words, codes, rt, lhs, rhs, total)
    out[...] = total[...]


def close_early(x):
    parts, powers = encode(x)
    powers.append(jnp.zeros((pad - len(powers), lane), f32))
    return whole(jnp.concatenate(parts + powers, axis=0))


def open_early(x, rows, across):
    at = rows * across
    return decode(x, rows, x[at : at + across])


def open_late(x, rows, across, groups):
    at = rows * across
    low, high = x[at : at + (x.shape[0] - at) // 2], x[at + (x.shape[0] - at) // 2 :]
    powers = low[groups * 10 : groups * 10 + across]
    return decode(x, rows, powers), jnp.concatenate([decode_sums(low, groups), decode_sums(high, groups)], axis=1)


def add_half_kernel(groups, own_late, own_sums, got, *outs):
    me = lax.axis_index("dp")
    n = len(outs)
    late, block, size = own_late.shape[0] // n, own_sums.shape[0] // n, got.shape[0] // n
    across = own_late.shape[1] // lane
    for i, k in enumerate((0,) + hops):
        cross, sums = open_late(got[k * size : (k + 1) * size, :].astype(f32), late, across, groups)
        parts, powers = encode(own_late[k * late : (k + 1) * late, :] + cross)
        sums += own_sums[pl.ds(pl.multiple_of((me ^ k) * block, 16), block), :]
        low, high = tiles(encode_sums(sums, groups))
        outs[i][...] = whole(jnp.concatenate(parts + [with_rows(low, powers, groups), high], axis=0))


def add_early_kernel(own, *rest):
    total = own[...]
    rows = total.shape[0]
    for q in rest[:-1]:
        total += open_early(q[...].astype(f32), rows, total.shape[1] // lane)
    rest[-1][...] = close_early(total)


def add_late_kernel(groups, late, across, *refs):
    cross = sums = None
    for q in refs[:-1]:
        c, s = open_late(q[...].astype(f32), late, across, groups)
        cross, sums = (c, s) if cross is None else (cross + c, sums + s)
    parts, powers = encode(cross)
    low, high = tiles(encode_sums(sums, groups))
    refs[-1][...] = whole(jnp.concatenate(parts + [with_rows(low, powers, groups), high], axis=0))


def finish_kernel(scale, *refs):
    mine, other, (codebook, out, cross, turned) = refs[:4], refs[4:8], refs[8:]
    width = codebook.shape[1]
    half = width // 2
    across = half // lane
    early = cross.shape[0] // 2
    late = early // 2
    core = lax.axis_index("replica") % 2
    low = lax.axis_index("replica") < 2
    groups = half // (8 * pack) // 2
    for start, (a0, a1, b0, b1) in ((core * half, mine), (half - core * half, other)):
        cols = pl.ds(pl.multiple_of(start, lane), half)
        total = open_early(a0[...].astype(f32), early, across) + open_early(a1[...].astype(f32), early, across)
        cross[:early, cols] = total * scale
        lates, halves = zip(*(open_late(b[...].astype(f32), late, across, groups) for b in (b0, b1)))
        for part, (a, b) in enumerate((lates, lates[::-1])):
            cross[early + part * late : early + (part + 1) * late, cols] = jnp.where(low, a, b) * scale
        for part, (a, b) in enumerate((halves, halves[::-1])):
            x = jnp.where(low, a, b)
            for g in range(groups):
                sums = x[g * 8 : g * 8 + 8]
                row = groups * 9 + g
                counts = jnp.broadcast_to(x[row : row + 1], sums.shape)
                for i in range(pack):
                    to = ((part * groups + g) * pack + i) * 8
                    cut = slice(i * fine, (i + 1) * fine)
                    turned[to : to + 8, :] = jnp.concatenate([sums[:, cut], counts[:, cut]], axis=1)
        t = turned[...].T
        old = codebook[:, cols].astype(f32)
        out[:, cols] = (t[:fine] + prior_count * old) / (t[fine:] + prior_count)


def local(embeddings, codes, rotation, codebook):
    rows, width = embeddings.shape
    n_sub = codes.shape[1]
    half = width // 2
    n = lax.axis_size("dp")
    replicas = lax.axis_size("replica")
    n_words = codebook.shape[0] * n
    owned = codebook.shape[0]
    out_rows = width // n
    direct = n == 4 and owned == fine and replicas == 4 and rows * n * replicas < 32768

    def swap(x, bit):
        return lax.ppermute(x, "replica", [(i, i ^ bit) for i in range(replicas)])

    def exchange(blocks, order):
        return [lax.ppermute(blocks[hops.index(k)], "dp", [(i, i ^ k) for i in range(n)]) for k in order]

    e1 = swap(embeddings, 1)
    c0 = codes.T
    c1 = swap(c0, 1)
    blank = call(blank_kernel, jax.ShapeDtypeStruct((8, lane), f32), (), [], "blank", flops=1 << 34)
    book = call(
        take_half_kernel,
        jax.ShapeDtypeStruct((owned, half), bf16),
        (codebook, blank),
        [],
        "take_half",
        flops=1 << 34,
        unread=(1,),
    )
    if direct:
        books = [book] + exchange([book] * len(hops), book_order)
    else:
        books = [lax.all_gather(book, "dp", axis=0, tiled=True)]
    n_out = n if direct else 1
    coarse = n_words // fine
    groups = n_sub // 2 // pack // 2
    block = block_rows(groups)
    lhs_rows = coarse * pack * 8 + 16
    sums_shape = (coarse * block, pack * fine)
    buffers = [
        pltpu.VMEM((2, lhs_rows, 2 * rows), bf16),
        pltpu.VMEM((2, pack * fine, 2 * rows), bf16),
        pltpu.VMEM(sums_shape, f32),
    ]
    first, my_codes, rt = call(
        lambda *refs: begin_kernel((rows, half, n_words, n_out), *refs),
        [
            jax.ShapeDtypeStruct(sums_shape, f32),
            jax.ShapeDtypeStruct((n_sub // 2, 2 * rows), i32),
            jax.ShapeDtypeStruct((half, 2 * rows), bf16),
        ],
        (c0, c1, embeddings, e1, rotation),
        buffers,
        "begin",
        flops=8 * rows * half * width,
    )
    early, late = out_rows // 2, out_rows // 4
    across = half // lane
    late_size = late * across + block * pack * fine // lane
    if direct:
        cross_outs = [
            jax.ShapeDtypeStruct((early, half), f32),
            jax.ShapeDtypeStruct((n * late, half), f32),
            jax.ShapeDtypeStruct((n * late_size, lane), i16),
        ] + [jax.ShapeDtypeStruct((early * across + pad, lane), i16)] * (n - 1)
    else:
        cross_outs = [jax.ShapeDtypeStruct((width, half), f32), jax.ShapeDtypeStruct(first.shape, f32)]
    cross = call(
        lambda *refs: cross_kernel((rows, half, n_words, len(books), n_out), *refs),
        cross_outs,
        (embeddings, e1, my_codes, first, *books),
        [
            pltpu.VMEM((n_words, half), f32),
            pltpu.VMEM((half, 2 * rows), bf16),
            pltpu.VMEM((width, half), f32),
        ],
        "cross_terms",
        flops=4 * rows * half * width,
    )
    scale = 1.0 / (rows * n * replicas)
    own = call(
        lambda *refs: sums_kernel((n_words, direct), *refs),
        jax.ShapeDtypeStruct(sums_shape, f32),
        (my_codes, rt, cross[0]),
        buffers,
        "codeword_sums",
        flops=8 * rows * half * width,
        unread=(2,),
    )
    if not direct:
        return plain_finish((cross[1], own), cross[0], codebook, n_words, scale, swap)

    own_early, own_late, message, *early_sent = cross
    late_blocks = call(
        lambda *refs: add_half_kernel(groups, *refs),
        [jax.ShapeDtypeStruct((late_size, lane), i16)] * n,
        (own_late, own, swap(message, 2)),
        [],
        "add_half",
    )
    a = call(
        add_early_kernel,
        jax.ShapeDtypeStruct((early * across + pad, lane), i16),
        (own_early, *exchange(early_sent, early_order)),
        [],
        "add_early",
    )
    b = call(
        lambda *refs: add_late_kernel(groups, late, across, *refs),
        jax.ShapeDtypeStruct((late_size, lane), i16),
        (late_blocks[0], *exchange(late_blocks[1:], late_order)),
        [],
        "add_late",
    )
    mine = (a, swap(a, 2), b, swap(b, 2))
    return call(
        lambda *refs: finish_kernel(scale, *refs),
        [jax.ShapeDtypeStruct(codebook.shape, f32), jax.ShapeDtypeStruct((out_rows, width), f32)],
        (*mine, *(swap(x, 1) for x in mine), codebook),
        [pltpu.VMEM((half, lane), f32)],
        "finish",
    )


def plain_finish(sums, cross, codebook, n_words, scale, swap):
    half = cross.shape[1]
    coarse = n_words // fine
    groups = half // (8 * pack) // 2
    sums = jnp.stack([x.reshape(coarse, -1, pack * fine) for x in sums])
    counts = sums[:, :, groups * 9 : groups * 10].reshape(2, coarse, groups, pack, fine)
    counts = counts.transpose(1, 4, 0, 2, 3).reshape(n_words, half // 8)
    sums = sums[:, :, : groups * 8].reshape(2, coarse, groups, 8, pack, fine)
    sums = sums.transpose(1, 5, 0, 2, 4, 3).reshape(n_words, half)
    parts = []
    for x in (sums, counts, cross):
        x = lax.psum_scatter(x, "dp", scatter_dimension=0, tiled=True)
        bit = 2
        while bit < lax.axis_size("replica"):
            x = x + swap(x, bit)
            bit *= 2
        y = swap(x, 1)
        first = lax.axis_index("replica") % 2 == 0
        parts.append(jnp.where(first, jnp.concatenate([x, y], 1), jnp.concatenate([y, x], 1)))
    sums, counts, cross = parts
    spread = jnp.repeat(counts, 8, axis=1)
    new_codebook = (sums + prior_count * codebook.astype(f32)) / (spread + prior_count)
    return new_codebook, cross * scale


def solution(mesh):
    in_specs = (
        P(("groups", "dp", "replica"), None),
        P(("groups", "dp", "replica"), None),
        P("groups", None),
        P(("groups", "dp"), None),
    )
    out_specs = (P(("groups", "dp"), None), P(("groups", "dp"), None))
    return jax.shard_map(local, mesh=mesh, in_specs=in_specs, out_specs=out_specs, check_vma=False)
```
